32 devices in a mesh: tm: 4 (over z), space: 8 (over y, x, core).
Axes of the slice: x: 2, y: 2, z: 4, core: 2. Of those that a mesh axis runs over, the one named last changes fastest.
Arguments:
- forcing: float32 [64, 3, 16, 8, 128], P('tm', None, 'space'), may hold values from -6 to 6
- start_field: float32 [3, 16, 8, 128], P(None, 'space'), may hold values from -6 to 6
- iterate: float32 [64, 3, 16, 8, 128], P('tm', None, 'space'), may hold values from -12 to 12
- region: int32 [16, 8, 128], P('space'), may hold values from 0 to 2
- conductance: float32 [3], replicated, may hold values from 0.5 to 4
Outputs:
- updated: float32 [64, 3, 16, 8, 128], P('tm', None, 'space')
The draws below stay inside these ranges and needn't reach their ends.
All inputs are finite; a program needn't handle non-finite values.
Results may differ from the reference program's by a relative error of at most 0.00013.
Values sent between devices are 32-bit elements; how exact they have to be, the bound alone decides.
A program may use at most 64 MiB of HBM per device.

```python
import math
import jax
import jax.numpy as jnp
from jax import lax

WINDOW = 64
NY = 8
NZ = 128
SWEEPS = 12
NX = 16


def with_ends(values, stream_key, least, top_value):
    extent = values.shape
    place = [jax.random.randint(jax.random.fold_in(stream_key, axis), (), 0, extent[axis]) for axis in range(len(extent))]
    values = values.at[tuple(place)].set(least)
    longest = extent.index(max(extent))
    place[longest] = (place[longest] + 1) % extent[longest]
    return values.at[tuple(place)].set(top_value)


def block_scale(rng, dims, split, smallest, top_value):
    loudness = 1.0
    for axis_at, parts in split:
        steps = jax.random.uniform(jax.random.fold_in(jax.random.fold_in(rng, 6), axis_at), (parts,), jnp.float32, smallest / len(split), top_value / len(split))
        loudness = loudness * jnp.repeat(jnp.exp(steps), dims[axis_at] // parts).reshape((-1,) + (1,) * (len(dims) - 1 - axis_at))
    return loudness


def gaussian(stream_key, dims, spread, limit, cuts=(), dtype=jnp.bfloat16):
    array = spread * jax.random.normal(stream_key, dims, jnp.float32)
    if cuts:
        array = array * block_scale(stream_key, dims, cuts, -0.22, 0.18)
    return jnp.clip(array, -limit, limit).astype(dtype)


def setup_inputs(seed: int = 0) -> dict:
    arg_keys = jax.random.split(jax.random.key(seed), 6)
    return {
        "forcing": gaussian(arg_keys[0], (WINDOW, 3, NX, NY, NZ), 1.0, 6.0, ((0, 4), (2, 8)), jnp.float32),
        "start_field": gaussian(arg_keys[1], (3, NX, NY, NZ), 1.0, 6.0, ((1, 8),), jnp.float32),
        "iterate": gaussian(arg_keys[2], (WINDOW, 3, NX, NY, NZ), 2.0, 12.0, ((0, 4), (2, 8)), jnp.float32),
        "region": with_ends(jax.random.randint(arg_keys[3], (NX, NY, NZ), 0, 3), jax.random.fold_in(arg_keys[3], 1), 0, 2).astype(jnp.int32),
        "conductance": jnp.clip(jnp.exp(jax.random.uniform(arg_keys[4], (3,), jnp.float32, math.log(0.5), math.log(4.0))), 0.5, 4.0),
    }


ALPHA = 0.1
LOWER = 0.02
UPPER = 1.0
SIGMA_TOP = 4.0
CURL_TOP = 12.0

def forward_step(values, axis):
    inner = lax.slice_in_dim(values, 1, values.shape[axis], axis=axis)
    border = jnp.zeros_like(lax.slice_in_dim(values, 0, 1, axis=axis))
    return jnp.concatenate([inner, border], axis) - values

def backward_step(values, axis):
    inner = lax.slice_in_dim(values, 0, values.shape[axis] - 1, axis=axis)
    border = jnp.zeros_like(lax.slice_in_dim(values, 0, 1, axis=axis))
    return jnp.concatenate([border, inner], axis) - values

def curl_forward(field):
    field_x, field_y, field_z = (field[:, 0], field[:, 1], field[:, 2])
    lead_x, lead_y, lead_z = (field_x[:, :-1], field_y[:, :-1], field_z[:, :-1])
    flux_x = forward_step(lead_z, 2) - forward_step(lead_y, 3)
    flux_y = forward_step(lead_x, 3) - (field_z[:, 1:] - field_z[:, :-1])
    flux_z = field_y[:, 1:] - field_y[:, :-1] - forward_step(lead_x, 2)
    return jnp.stack([flux_x, flux_y, flux_z], axis=1)

def curl_adjoint(flux):
    flux_x, flux_y, flux_z = (flux[:, 0], flux[:, 1], flux[:, 2])
    tail_x, tail_y, tail_z = (flux_x[:, 1:], flux_y[:, 1:], flux_z[:, 1:])
    field_x = backward_step(tail_y, 3) - backward_step(tail_z, 2)
    field_y = flux_z[:, :-1] - flux_z[:, 1:] - backward_step(tail_x, 3)
    field_z = backward_step(tail_x, 2) - (flux_y[:, :-1] - flux_y[:, 1:])
    return jnp.stack([field_x, field_y, field_z], axis=1)

def full_curl(field):
    plane = jnp.zeros_like(field[:, :, :1])
    flux = curl_forward(jnp.concatenate([field, plane], 2))
    return curl_adjoint(jnp.concatenate([jnp.zeros_like(flux[:, :, :1]), flux], 2))

def pair_terms(pairs, window):
    gamma = ALPHA ** (1.0 / window)
    angle = 2.0 * math.pi * pairs.astype(jnp.float32) / window
    plain = 1.0 - gamma * jnp.cos(angle)
    p_plus = jnp.where(pairs == 0, 1.0 - gamma, plain)
    p_minus = jnp.where(pairs == 0, 1.0 + gamma, plain)
    q_term = jnp.where(pairs == 0, 0.0, gamma * jnp.sin(angle))
    bound = jnp.sqrt(jnp.maximum(p_plus, p_minus) ** 2 + q_term ** 2) * SIGMA_TOP + CURL_TOP
    return (p_plus, p_minus, q_term, bound * bound)

def cas_rows(freqs, window):
    moments = jnp.arange(window).astype(jnp.int32)
    product = freqs[:, None] * moments[None, :] % window
    angle = 2.0 * math.pi * product.astype(jnp.float32) / window
    return jnp.cos(angle) + jnp.sin(angle)

def powers(window, sign):
    gamma = jnp.float32(ALPHA ** (sign / window))
    return jnp.power(gamma, jnp.arange(window).astype(jnp.float32))

def chebyshev_terms(count):
    center = (UPPER + LOWER) / 2.0
    radius = (UPPER - LOWER) / 2.0
    spread_ratio = center / radius
    weight_now = 1.0 / spread_ratio
    carry_terms, push_terms = ([], [])
    for _ in range(count):
        weight_next = 1.0 / (2.0 * spread_ratio - weight_now)
        carry_terms.append(weight_next * weight_now)
        push_terms.append(2.0 * weight_next / radius)
        weight_now = weight_next
    return (jnp.asarray(carry_terms, jnp.float32), jnp.asarray(push_terms, jnp.float32), center)

def reference(forcing, start_field, iterate, region, conductance):
    window = forcing.shape[0]
    half = window // 2
    sigma = jnp.zeros(region.shape, jnp.float32)
    for material in range(3):
        sigma = sigma + conductance[material] * (region == material).astype(jnp.float32)
    jump = sigma * (start_field - ALPHA * iterate[window - 1])
    rhs = forcing.at[0].add(jump)
    cells = rhs[0].size
    flat = rhs.reshape(window, cells)
    pairs = jnp.arange(half).astype(jnp.int32)
    k_plus = pairs
    k_minus = jnp.where(pairs == 0, half, window - pairs).astype(jnp.int32)
    grow = powers(window, 1.0)
    shrink = powers(window, -1.0)
    spec_plus = jnp.dot(cas_rows(k_plus, window) * grow[None, :], flat, precision=lax.Precision.HIGHEST)
    spec_minus = jnp.dot(cas_rows(k_minus, window) * grow[None, :], flat, precision=lax.Precision.HIGHEST)
    p_plus, p_minus, q_term, scale = pair_terms(pairs, window)
    carry_terms, push_terms, center = chebyshev_terms(SWEEPS - 1)
    shape = (2,) + forcing.shape[1:]

    def solve_pair(items):
        rhs_plus, rhs_minus, plus_coef, minus_coef, cross, norm_scale = items
        stacked = jnp.stack([rhs_plus, rhs_minus]).reshape(shape)
        diagonal_coef = jnp.stack([plus_coef, minus_coef]).reshape(2, 1, 1, 1, 1)

        def couple(values, sign):
            swapped = jnp.stack([-cross * values[1], cross * values[0]])
            return sigma * (diagonal_coef * values + sign * swapped)

        def normal(values):
            first = full_curl(values) + couple(values, 1.0)
            return (full_curl(first) + couple(first, -1.0)) / norm_scale
        start = (full_curl(stacked) + couple(stacked, -1.0)) / norm_scale

        def sweep(sweep_index, carry_state):
            current, residual, direction = carry_state
            current = current + direction
            residual = residual - normal(direction)
            direction = carry_terms[sweep_index] * direction + push_terms[sweep_index] * residual
            return (current, residual, direction)
        current, residual, direction = lax.fori_loop(0, SWEEPS - 1, sweep, (jnp.zeros_like(start), start, start / center))
        result = (current + direction).reshape(2, cells)
        return (result[0], result[1])
    sol_plus, sol_minus = lax.map(solve_pair, (spec_plus, spec_minus, p_plus, p_minus, q_term, scale))
    back_plus = cas_rows(k_plus, window).T * (shrink / window)[:, None]
    back_minus = cas_rows(k_minus, window).T * (shrink / window)[:, None]
    updated = jnp.dot(back_plus, sol_plus, precision=lax.Precision.HIGHEST) + jnp.dot(back_minus, sol_minus, precision=lax.Precision.HIGHEST)
    return updated.reshape(forcing.shape)
```

```python
import math

import functools

import jax
import jax.numpy as jnp
import numpy as np
from jax import lax
from jax.experimental import pallas as pl
from jax.experimental.pallas import tpu as pltpu
from jax.sharding import PartitionSpec as P

SWEEPS = 12


ALPHA = 0.1
LOWER = 0.02
UPPER = 1.0
SIGMA_TOP = 4.0
CURL_TOP = 12.0


def from_behind(value, axis, steps):
    count = lax.axis_size(axis)
    initial, last = (max(0, -steps), min(count, count - steps))
    return lax.ppermute(value, axis, [(source, source + steps) for source in range(initial, last)])


def broadcast(array, axis, root):
    mine = lax.axis_index(axis) == root
    return lax.psum(jnp.where(mine, array, jnp.zeros_like(array)), axis)


def forward_step(values, axis):
    inner = lax.slice_in_dim(values, 1, values.shape[axis], axis=axis)
    border = jnp.zeros_like(lax.slice_in_dim(values, 0, 1, axis=axis))
    return jnp.concatenate([inner, border], axis) - values


def backward_step(values, axis):
    inner = lax.slice_in_dim(values, 0, values.shape[axis] - 1, axis=axis)
    border = jnp.zeros_like(lax.slice_in_dim(values, 0, 1, axis=axis))
    return jnp.concatenate([border, inner], axis) - values


def curl_forward(field):
    field_x, field_y, field_z = (field[:, 0], field[:, 1], field[:, 2])
    lead_x, lead_y, lead_z = (field_x[:, :-1], field_y[:, :-1], field_z[:, :-1])
    flux_x = forward_step(lead_z, 2) - forward_step(lead_y, 3)
    flux_y = forward_step(lead_x, 3) - (field_z[:, 1:] - field_z[:, :-1])
    flux_z = field_y[:, 1:] - field_y[:, :-1] - forward_step(lead_x, 2)
    return jnp.stack([flux_x, flux_y, flux_z], axis=1)


def curl_adjoint(flux):
    flux_x, flux_y, flux_z = (flux[:, 0], flux[:, 1], flux[:, 2])
    tail_x, tail_y, tail_z = (flux_x[:, 1:], flux_y[:, 1:], flux_z[:, 1:])
    field_x = backward_step(tail_y, 3) - backward_step(tail_z, 2)
    field_y = flux_z[:, :-1] - flux_z[:, 1:] - backward_step(tail_x, 3)
    field_z = backward_step(tail_x, 2) - (flux_y[:, :-1] - flux_y[:, 1:])
    return jnp.stack([field_x, field_y, field_z], axis=1)


def brick_curl(field):
    upper = from_behind(field[:, :, :1], "space", -1)
    flux = curl_forward(jnp.concatenate([field, upper], 2))
    lower = from_behind(flux[:, :, -1:], "space", 1)
    return curl_adjoint(jnp.concatenate([lower, flux], 2))


def pair_terms(pairs, window):
    gamma = ALPHA ** (1.0 / window)
    angle = 2.0 * math.pi * pairs.astype(jnp.float32) / window
    plain = 1.0 - gamma * jnp.cos(angle)
    p_plus = jnp.where(pairs == 0, 1.0 - gamma, plain)
    p_minus = jnp.where(pairs == 0, 1.0 + gamma, plain)
    q_term = jnp.where(pairs == 0, 0.0, gamma * jnp.sin(angle))
    bound = jnp.sqrt(jnp.maximum(p_plus, p_minus) ** 2 + q_term**2) * SIGMA_TOP + CURL_TOP
    return (p_plus, p_minus, q_term, bound * bound)


def cas_table(freqs, window):
    moments = jnp.arange(window)
    product = freqs[:, None] * moments[None, :] % window
    angle = 2.0 * math.pi * product.astype(jnp.float32) / window
    return jnp.cos(angle) + jnp.sin(angle)


def powers(window, sign):
    gamma = jnp.float32(ALPHA ** (sign / window))
    return jnp.power(gamma, jnp.arange(window).astype(jnp.float32))


def frequency_order(window, steps):
    slots = jnp.arange(window)
    half = steps // 2
    within = slots % steps
    pairs = slots // steps * half + within % half
    mirror = jnp.where(pairs == 0, window // 2, window - pairs)
    return jnp.where(within < half, pairs, mirror)


def chebyshev_terms(count):
    center = (UPPER + LOWER) / 2.0
    radius = (UPPER - LOWER) / 2.0
    spread_ratio = center / radius
    weight_now = 1.0 / spread_ratio
    carry_terms, push_terms = ([], [])
    for _ in range(count):
        weight_next = 1.0 / (2.0 * spread_ratio - weight_now)
        carry_terms.append(weight_next * weight_now)
        push_terms.append(2.0 * weight_next / radius)
        weight_now = weight_next
    return (jnp.asarray(carry_terms, jnp.float32), jnp.asarray(push_terms, jnp.float32), center)


def per_device(forcing, start_field, iterate, region, conductance):
    steps = forcing.shape[0]
    half = steps // 2
    groups = lax.axis_size("tm")
    window = steps * groups
    depth_z = forcing.shape[4]
    sigma = jnp.zeros(region.shape, jnp.float32)
    for material in range(3):
        sigma = sigma + conductance[material] * (region == material).astype(jnp.float32)
    order = frequency_order(window, steps)
    forward_table = cas_table(order, window) * powers(window, 1.0)[None, :]
    inverse_table = cas_table(order, window).T * (powers(window, -1.0) / window)[:, None]
    flat = forcing.reshape(steps, groups, -1, depth_z)
    spread = jnp.einsum(
        "kn,ngrz->kgrz",
        forward_table,
        lax.all_to_all(flat, "tm", split_axis=1, concat_axis=0, tiled=True),
        precision=lax.Precision.HIGHEST,
    )
    spectrum = lax.all_to_all(spread, "tm", split_axis=0, concat_axis=1, tiled=True).reshape(
        forcing.shape
    )
    latest = broadcast(iterate[steps - 1], "tm", lax.axis_size("tm") - 1)
    spectrum = spectrum + (sigma * (start_field - ALPHA * latest))[None]
    pairs = lax.axis_index("tm") * half + jnp.arange(half)
    p_plus, p_minus, q_term, scale = pair_terms(pairs, window)
    diagonal_coef = jnp.concatenate([p_plus, p_minus]).reshape(steps, 1, 1, 1, 1)
    cross = q_term.reshape(half, 1, 1, 1, 1)
    norm_scale = jnp.concatenate([scale, scale]).reshape(steps, 1, 1, 1, 1)

    def couple(values, sign, weights):
        swapped = jnp.concatenate([-cross * values[half:], cross * values[:half]], 0)
        return weights * (diagonal_coef * values + sign * swapped)

    def normal(values):
        first = brick_curl(values) + couple(values, 1.0, sigma)
        return (brick_curl(first) + couple(first, -1.0, sigma)) / norm_scale

    start = (brick_curl(spectrum) + couple(spectrum, -1.0, sigma)) / norm_scale
    carry_terms, push_terms, center = chebyshev_terms(SWEEPS - 1)

    def sweep(sweep_index, carry_state):
        current, residual, direction = carry_state
        current = current + direction
        residual = residual - normal(direction)
        direction = carry_terms[sweep_index] * direction + push_terms[sweep_index] * residual
        return (current, residual, direction)

    current, residual, direction = lax.fori_loop(
        0, SWEEPS - 1, sweep, (jnp.zeros_like(start), start, start / center)
    )
    solution = (current + direction).reshape(steps, groups, -1, depth_z)
    spread_back = jnp.einsum(
        "nk,kgrz->ngrz",
        inverse_table,
        lax.all_to_all(solution, "tm", split_axis=1, concat_axis=0, tiled=True),
        precision=lax.Precision.HIGHEST,
    )
    updated = lax.all_to_all(spread_back, "tm", split_axis=0, concat_axis=1, tiled=True)
    return updated.reshape(forcing.shape)


CHUNKS = 6


def pair_numbers(window, groups, spots):
    table = np.zeros((groups, spots), np.int64)
    for z in range(groups):
        for s in range(spots):
            table[z, s] = 2 * (spots * (z % 2) + s) + z // 2
    return table


def host_tables(window, groups, spots):
    steps = window // groups
    gamma = ALPHA ** (1.0 / window)
    pairs = pair_numbers(window, groups, spots)
    cas = lambda k, n: np.cos(2 * np.pi * ((k * n) % window) / window) + np.sin(
        2 * np.pi * ((k * n) % window) / window
    )
    rows = np.arange(steps)
    merge = np.zeros((groups, 2, steps))
    split = np.zeros((groups, 2, steps))
    ahead = np.zeros((groups, spots, 2, 2, steps))
    back = np.zeros((groups, 2, steps, spots, 2))
    last = np.zeros((groups, 2))
    for z in range(groups):
        mine, other = steps * z + rows, steps * ((z + 2) % 4) + rows
        upper = z // 2
        merge[z, 0] = (-1.0 if upper else 1.0) * gamma**mine
        merge[z, 1] = gamma**other
        split[z, 0] = (-1.0 if upper else 1.0) * gamma**-mine / window
        split[z, 1] = gamma**-mine / window
        for s in range(spots):
            j = pairs[z, s]
            for f, k in enumerate((j, window // 2 if j == 0 else window - j)):
                for side, low in enumerate((z % 2, 1 - z % 2)):
                    ahead[z, s, f, side] = cas(k, steps * low + rows)
                    back[z, side, :, s, f] = cas(k, steps * low + rows)
    last[1, 1] = 1.0
    last[3, 0] = 1.0
    theta = 2 * np.pi * pairs / window
    plain = 1 - gamma * np.cos(theta)
    p_plus = np.where(pairs == 0, 1 - gamma, plain)
    p_minus = np.where(pairs == 0, 1 + gamma, plain)
    cross = np.where(pairs == 0, 0.0, gamma * np.sin(theta))
    scale = (np.sqrt(np.maximum(p_plus, p_minus) ** 2 + cross**2) * SIGMA_TOP + CURL_TOP) ** 2
    coef = np.stack([p_plus, p_minus, cross, 1 / scale], -1)
    center, radius = (UPPER + LOWER) / 2, (UPPER - LOWER) / 2
    now, cheb = radius / center, []
    for _ in range(SWEEPS - 1):
        later = 1.0 / (2.0 * center / radius - now)
        cheb += [later * now, 2.0 * later / radius]
        now = later
    flat = lambda value: np.asarray(value, np.float32).reshape(-1)
    return [flat(v) for v in (merge, ahead, last, coef, cheb, back, split)], 1 / center


def window_kernel(
    steps, spots, inverse_center,
    merge, ahead, last, coef, cheb, back, split, conductance,
    force, start, region, iterate, out,
    got_last, got_far, mixed, got_near, extra, got_extra, mine_freq, spec, sigma,
    first, res, step, total, home, half, got_half, even, got_even,
    last_sem, far_sem, near_sem, extra_sem, sigma_sem, spec_sem, home_sem, half_sem, even_sem,
):
    z, s = lax.axis_index("tm"), lax.axis_index("space")
    far = ((z + 2) % 4, s)
    near = (z + 1 - 2 * (z % 2), s)
    peers = [(z, (s + hop) % spots) for hop in range(1, spots)]
    width = 6 // CHUNKS
    planes = 2 * spots
    parts = [pl.ds(c * width, width) for c in range(CHUNKS)]
    sent = []

    def send(source, target, sems, slot, device):
        copy = pltpu.make_async_remote_copy(
            src_ref=source, dst_ref=target,
            send_sem=sems.at[(0,) + slot], recv_sem=sems.at[(1,) + slot],
            device_id=device, device_id_type=pl.DeviceIdType.MESH,
        )
        copy.start()
        sent.append(copy)
        return copy

    barrier = pltpu.get_barrier_semaphore()
    for device in [far, near] + peers:
        pl.semaphore_signal(barrier, inc=1, device_id=device, device_id_type=pl.DeviceIdType.MESH)

    material = region[...]
    brick_sigma = jnp.zeros(material.shape, jnp.float32)
    for index in range(3):
        brick_sigma = brick_sigma + jnp.where(material == index, conductance[index], 0.0)
    sigma[s] = brick_sigma
    pl.semaphore_wait(barrier, 2 + len(peers))

    last_copy = send(iterate.at[steps - 1], got_last, last_sem, (0,), far)
    far_copies = [
        send(force.at[:, part], got_far.at[:, part], far_sem, (c,), far)
        for c, part in enumerate(parts)
    ]
    sigma_copies = [
        send(sigma.at[s], sigma.at[s], sigma_sem, (h,), peer) for h, peer in enumerate(peers)
    ]
    last_copy.wait_recv()
    extra[...] = last[z * 2] * iterate[steps - 1] + last[z * 2 + 1] * got_last[...]
    extra_copy = send(extra, got_extra, extra_sem, (0,), near)

    def mix(c):
        far_copies[c].wait_recv()

        def row(m, carry):
            w_mine, w_other = merge[z * 2 * steps + m], merge[(z * 2 + 1) * steps + m]
            for t in range(c * width, (c + 1) * width):
                mixed[m, t] = w_mine * force[m, t] + w_other * got_far[m, t]
            return carry

        lax.fori_loop(0, steps, row, 0, unroll=4)
        return send(mixed.at[:, parts[c]], got_near.at[:, parts[c]], near_sem, (c,), near)

    spec_copies = [None] * CHUNKS

    def transform(c, copy):
        copy.wait_recv()
        if c == 0:
            extra_copy.wait_recv()
            got_extra[...] = start[...] - ALPHA * (extra[...] + got_extra[...])
        jump = [brick_sigma[t % 2] * got_extra[t] for t in range(c * width, (c + 1) * width)]

        def slot(k, carry):
            base = (z * 2 * spots + k) * 2 * steps
            sums = [[j, None] for j in jump]
            for m in range(steps):
                w_mine, w_other = ahead[base + m], ahead[base + steps + m]
                for i in range(width):
                    t = c * width + i
                    term = w_other * got_near[m, t]
                    sums[i][0] = sums[i][0] + w_mine * mixed[m, t]
                    sums[i][1] = term if m == 0 else sums[i][1] + term
            for i in range(width):
                mine_freq[k // 2, c * width + i, k % 2] = sums[i][0] + sums[i][1]
            return carry

        lax.fori_loop(0, 2 * spots, slot, 0)
        spec[s, parts[c]] = mine_freq[s, parts[c]]
        spec_copies[c] = [
            send(mine_freq.at[peer[1], parts[c]], spec.at[s, parts[c]], spec_sem, (c, h), peer)
            for h, peer in enumerate(peers)
        ]

    pending = mix(0)
    for c in range(CHUNKS):
        later = mix(c + 1) if c + 1 < CHUNKS else None
        transform(c, pending)
        pending = later
    for copy in sigma_copies + [copy for group in spec_copies for copy in group]:
        copy.wait_recv()

    device = z * spots + s
    p_plus, p_minus = coef[device * 4], coef[device * 4 + 1]
    cross, inverse_scale = coef[device * 4 + 2], coef[device * 4 + 3]
    along_y = lax.broadcasted_iota(jnp.int32, (8, 128), 0)
    along_z = lax.broadcasted_iota(jnp.int32, (8, 128), 1)
    not_top_y, not_top_z = along_y < 7, along_z < 127
    not_low_y, not_low_z = along_y > 0, along_z > 0
    zero = jnp.zeros((8, 128), jnp.float32)

    def up_y(v):
        return jnp.where(not_top_y, pltpu.roll(v, 7, 0), 0.0)

    def up_z(v):
        return jnp.where(not_top_z, pltpu.roll(v, 127, 1), 0.0)

    def down_y(v):
        return jnp.where(not_low_y, pltpu.roll(v, 1, 0), 0.0)

    def down_z(v):
        return jnp.where(not_low_z, pltpu.roll(v, 1, 1), 0.0)

    def operator(buffer, sign, finish):
        load = lambda i: [[buffer[i // 2, 2 * e + i % 2, f] for e in range(3)] for f in range(2)]
        here = load(0)
        behind = [(zero, zero), (zero, zero)]
        for i in range(planes):
            ahead_field = load(i + 1) if i + 1 < planes else [[zero] * 3] * 2
            weight = sigma[i // 2, i % 2]
            weights = (weight * p_plus, weight * p_minus)
            weight_cross = weight * cross
            for f in range(2):
                ex, ey, ez = here[f]
                _, ey1, ez1 = ahead_field[f]
                bx = (up_y(ez) - ez) - (up_z(ey) - ey)
                by = (up_z(ex) - ex) - (ez1 - ez)
                bz = (ey1 - ey) - (up_y(ex) - ex)
                by0, bz0 = behind[f]
                curls = (
                    (down_z(by) - by) - (down_y(bz) - bz),
                    (bz0 - bz) - (down_z(bx) - bx),
                    (down_y(bx) - bx) - (by0 - by),
                )
                behind[f] = (by, bz)
                for e in range(3):
                    own = weights[f] * here[f][e]
                    swapped = weight_cross * here[1 - f][e]
                    value = curls[e] + own
                    value = value + swapped if (f == 1) == (sign > 0) else value - swapped
                    finish(i, e, f, value)
            here = ahead_field

    def begin(i, e, f, value):
        at = (i // 2, 2 * e + i % 2, f)
        g = value * inverse_scale
        res[at] = g
        step[at] = g * inverse_center
        total[at] = zero

    operator(spec, -1.0, begin)

    def sweep(index, carry):
        w_step, w_res = cheb[index * 2], cheb[index * 2 + 1]

        def keep(i, e, f, value):
            first[i // 2, 2 * e + i % 2, f] = value

        def advance(i, e, f, value):
            at = (i // 2, 2 * e + i % 2, f)
            old = step[at]
            total[at] = total[at] + old
            new = res[at] - value * inverse_scale
            res[at] = new
            step[at] = w_step * old + w_res * new

        operator(step, 1.0, keep)
        operator(first, -1.0, advance)
        return carry

    lax.fori_loop(0, SWEEPS - 1, sweep, 0)

    home_copies = []
    for c, part in enumerate(parts):
        for b in range(spots):
            for t in range(c * width, (c + 1) * width):
                for f in range(2):
                    total[b, t, f] = total[b, t, f] + step[b, t, f]
        home[s, part] = total[s, part]
        home_copies.append([
            send(total.at[peer[1], part], home.at[s, part], home_sem, (c, h), peer)
            for h, peer in enumerate(peers)
        ])

    def gather(c):
        for copy in home_copies[c]:
            copy.wait_recv()

        def row(m, carry):
            base_mine = (z * 2 * steps + m) * 2 * spots
            base_other = ((z * 2 + 1) * steps + m) * 2 * spots
            for t in range(c * width, (c + 1) * width):
                mine, other = None, None
                for b in range(spots):
                    for f in range(2):
                        value = home[b, t, f]
                        term = back[base_mine + 2 * b + f] * value
                        mine = term if mine is None else mine + term
                        term = back[base_other + 2 * b + f] * value
                        other = term if other is None else other + term
                even[m, t] = mine
                half[m, t] = other
            return carry

        lax.fori_loop(0, steps, row, 0)
        return send(half.at[:, parts[c]], got_half.at[:, parts[c]], half_sem, (c,), near)

    def add(c, copy):
        copy.wait_recv()
        even[:, parts[c]] = even[:, parts[c]] + got_half[:, parts[c]]
        return send(even.at[:, parts[c]], got_even.at[:, parts[c]], even_sem, (c,), far)

    half_copies = [gather(0)]
    even_copies = []
    for c in range(CHUNKS):
        if c + 1 < CHUNKS:
            half_copies.append(gather(c + 1))
        even_copies.append(add(c, half_copies[c]))
    for c in range(CHUNKS):
        even_copies[c].wait_recv()

        def row(m, carry):
            w_mine, w_other = split[z * 2 * steps + m], split[(z * 2 + 1) * steps + m]
            for t in range(c * width, (c + 1) * width):
                out[m, t] = w_mine * even[m, t] + w_other * got_even[m, t]
            return carry

        lax.fori_loop(0, steps, row, 0, unroll=4)
    for copy in sent:
        copy.wait_send()


def pair_per_device(groups, spots, forcing, start_field, iterate, region, conductance):
    steps = forcing.shape[0]
    tables, inverse_center = host_tables(steps * groups, groups, spots)
    tile = forcing.shape[3:]
    f32 = jnp.float32
    brick = lambda *lead: pltpu.VMEM(lead + tile, f32)
    rows = brick(steps, 6)
    grid = brick(spots, 6, 2)
    dma = pltpu.SemaphoreType.DMA
    smem, vmem = pl.BlockSpec(memory_space=pltpu.SMEM), pl.BlockSpec(memory_space=pltpu.VMEM)
    result = pl.pallas_call(
        functools.partial(window_kernel, steps, spots, inverse_center),
        out_shape=jax.ShapeDtypeStruct((steps, 6) + tile, f32),
        in_specs=[smem] * 8 + [vmem] * 4,
        out_specs=vmem,
        scratch_shapes=[
            brick(6), rows, rows, rows, brick(6), brick(6), grid, grid, brick(spots, 2),
            grid, grid, grid, grid, grid, rows, rows, rows, rows,
            dma((2, 1)), dma((2, CHUNKS)), dma((2, CHUNKS)), dma((2, 1)), dma((2, spots - 1)),
            dma((2, CHUNKS, spots - 1)), dma((2, CHUNKS, spots - 1)),
            dma((2, CHUNKS)), dma((2, CHUNKS)),
        ],
        compiler_params=pltpu.CompilerParams(
            collective_id=0, has_side_effects=True, vmem_limit_bytes=32 * 1024 * 1024
        ),
    )(
        *[jnp.asarray(table) for table in tables], conductance,
        forcing.reshape((steps, 6) + tile), start_field.reshape((6,) + tile), region,
        iterate.reshape((steps, 6) + tile),
    )
    return result.reshape(forcing.shape)


def solution(mesh):
    placed = (
        P("tm", None, "space", None, None),
        P(None, "space", None, None),
        P("tm", None, "space", None, None),
        P("space", None, None),
        P(),
    )
    groups, spots = mesh.shape["tm"], mesh.shape["space"]

    def per_block(*arrays):
        steps, planes = arrays[0].shape[0], arrays[0].shape[2]
        one_each = steps * groups == 2 * groups * spots
        if groups == 4 and one_each and planes == 2 and arrays[0].shape[3:] == (8, 128):
            return pair_per_device(groups, spots, *arrays)
        return per_device(*arrays)

    return jax.shard_map(
        per_block,
        mesh=mesh,
        in_specs=placed,
        out_specs=P("tm", None, "space", None, None),
        check_vma=False,
    )
```

```python
import math

import functools

import jax
import jax.numpy as jnp
import numpy as np
from jax import lax
from jax.experimental import pallas as pl
from jax.experimental.pallas import tpu as pltpu
from jax.sharding import PartitionSpec as P

SWEEPS = 12


ALPHA = 0.1
LOWER = 0.02
UPPER = 1.0
SIGMA_TOP = 4.0
CURL_TOP = 12.0


def from_behind(value, axis, steps):
    count = lax.axis_size(axis)
    initial, last = (max(0, -steps), min(count, count - steps))
    return lax.ppermute(value, axis, [(source, source + steps) for source in range(initial, last)])


def broadcast(array, axis, root):
    mine = lax.axis_index(axis) == root
    return lax.psum(jnp.where(mine, array, jnp.zeros_like(array)), axis)


def forward_step(values, axis):
    inner = lax.slice_in_dim(values, 1, values.shape[axis], axis=axis)
    border = jnp.zeros_like(lax.slice_in_dim(values, 0, 1, axis=axis))
    return jnp.concatenate([inner, border], axis) - values


def backward_step(values, axis):
    inner = lax.slice_in_dim(values, 0, values.shape[axis] - 1, axis=axis)
    border = jnp.zeros_like(lax.slice_in_dim(values, 0, 1, axis=axis))
    return jnp.concatenate([border, inner], axis) - values


def curl_forward(field):
    field_x, field_y, field_z = (field[:, 0], field[:, 1], field[:, 2])
    lead_x, lead_y, lead_z = (field_x[:, :-1], field_y[:, :-1], field_z[:, :-1])
    flux_x = forward_step(lead_z, 2) - forward_step(lead_y, 3)
    flux_y = forward_step(lead_x, 3) - (field_z[:, 1:] - field_z[:, :-1])
    flux_z = field_y[:, 1:] - field_y[:, :-1] - forward_step(lead_x, 2)
    return jnp.stack([flux_x, flux_y, flux_z], axis=1)


def curl_adjoint(flux):
    flux_x, flux_y, flux_z = (flux[:, 0], flux[:, 1], flux[:, 2])
    tail_x, tail_y, tail_z = (flux_x[:, 1:], flux_y[:, 1:], flux_z[:, 1:])
    field_x = backward_step(tail_y, 3) - backward_step(tail_z, 2)
    field_y = flux_z[:, :-1] - flux_z[:, 1:] - backward_step(tail_x, 3)
    field_z = backward_step(tail_x, 2) - (flux_y[:, :-1] - flux_y[:, 1:])
    return jnp.stack([field_x, field_y, field_z], axis=1)


def brick_curl(field):
    upper = from_behind(field[:, :, :1], "space", -1)
    flux = curl_forward(jnp.concatenate([field, upper], 2))
    lower = from_behind(flux[:, :, -1:], "space", 1)
    return curl_adjoint(jnp.concatenate([lower, flux], 2))


def pair_terms(pairs, window):
    gamma = ALPHA ** (1.0 / window)
    angle = 2.0 * math.pi * pairs.astype(jnp.float32) / window
    plain = 1.0 - gamma * jnp.cos(angle)
    p_plus = jnp.where(pairs == 0, 1.0 - gamma, plain)
    p_minus = jnp.where(pairs == 0, 1.0 + gamma, plain)
    q_term = jnp.where(pairs == 0, 0.0, gamma * jnp.sin(angle))
    bound = jnp.sqrt(jnp.maximum(p_plus, p_minus) ** 2 + q_term**2) * SIGMA_TOP + CURL_TOP
    return (p_plus, p_minus, q_term, bound * bound)


def cas_table(freqs, window):
    moments = jnp.arange(window)
    product = freqs[:, None] * moments[None, :] % window
    angle = 2.0 * math.pi * product.astype(jnp.float32) / window
    return jnp.cos(angle) + jnp.sin(angle)


def powers(window, sign):
    gamma = jnp.float32(ALPHA ** (sign / window))
    return jnp.power(gamma, jnp.arange(window).astype(jnp.float32))


def frequency_order(window, steps):
    slots = jnp.arange(window)
    half = steps // 2
    within = slots % steps
    pairs = slots // steps * half + within % half
    mirror = jnp.where(pairs == 0, window // 2, window - pairs)
    return jnp.where(within < half, pairs, mirror)


def chebyshev_terms(count):
    center = (UPPER + LOWER) / 2.0
    radius = (UPPER - LOWER) / 2.0
    spread_ratio = center / radius
    weight_now = 1.0 / spread_ratio
    carry_terms, push_terms = ([], [])
    for _ in range(count):
        weight_next = 1.0 / (2.0 * spread_ratio - weight_now)
        carry_terms.append(weight_next * weight_now)
        push_terms.append(2.0 * weight_next / radius)
        weight_now = weight_next
    return (jnp.asarray(carry_terms, jnp.float32), jnp.asarray(push_terms, jnp.float32), center)


def per_device(forcing, start_field, iterate, region, conductance):
    steps = forcing.shape[0]
    half = steps // 2
    groups = lax.axis_size("tm")
    window = steps * groups
    depth_z = forcing.shape[4]
    sigma = jnp.zeros(region.shape, jnp.float32)
    for material in range(3):
        sigma = sigma + conductance[material] * (region == material).astype(jnp.float32)
    order = frequency_order(window, steps)
    forward_table = cas_table(order, window) * powers(window, 1.0)[None, :]
    inverse_table = cas_table(order, window).T * (powers(window, -1.0) / window)[:, None]
    flat = forcing.reshape(steps, groups, -1, depth_z)
    spread = jnp.einsum(
        "kn,ngrz->kgrz",
        forward_table,
        lax.all_to_all(flat, "tm", split_axis=1, concat_axis=0, tiled=True),
        precision=lax.Precision.HIGHEST,
    )
    spectrum = lax.all_to_all(spread, "tm", split_axis=0, concat_axis=1, tiled=True).reshape(
        forcing.shape
    )
    latest = broadcast(iterate[steps - 1], "tm", lax.axis_size("tm") - 1)
    spectrum = spectrum + (sigma * (start_field - ALPHA * latest))[None]
    pairs = lax.axis_index("tm") * half + jnp.arange(half)
    p_plus, p_minus, q_term, scale = pair_terms(pairs, window)
    diagonal_coef = jnp.concatenate([p_plus, p_minus]).reshape(steps, 1, 1, 1, 1)
    cross = q_term.reshape(half, 1, 1, 1, 1)
    norm_scale = jnp.concatenate([scale, scale]).reshape(steps, 1, 1, 1, 1)

    def couple(values, sign, weights):
        swapped = jnp.concatenate([-cross * values[half:], cross * values[:half]], 0)
        return weights * (diagonal_coef * values + sign * swapped)

    def normal(values):
        first = brick_curl(values) + couple(values, 1.0, sigma)
        return (brick_curl(first) + couple(first, -1.0, sigma)) / norm_scale

    start = (brick_curl(spectrum) + couple(spectrum, -1.0, sigma)) / norm_scale
    carry_terms, push_terms, center = chebyshev_terms(SWEEPS - 1)

    def sweep(sweep_index, carry_state):
        current, residual, direction = carry_state
        current = current + direction
        residual = residual - normal(direction)
        direction = carry_terms[sweep_index] * direction + push_terms[sweep_index] * residual
        return (current, residual, direction)

    current, residual, direction = lax.fori_loop(
        0, SWEEPS - 1, sweep, (jnp.zeros_like(start), start, start / center)
    )
    solution = (current + direction).reshape(steps, groups, -1, depth_z)
    spread_back = jnp.einsum(
        "nk,kgrz->ngrz",
        inverse_table,
        lax.all_to_all(solution, "tm", split_axis=1, concat_axis=0, tiled=True),
        precision=lax.Precision.HIGHEST,
    )
    updated = lax.all_to_all(spread_back, "tm", split_axis=0, concat_axis=1, tiled=True)
    return updated.reshape(forcing.shape)


CHUNKS = 3


def pair_numbers(window, groups, spots):
    table = np.zeros((groups, spots), np.int64)
    for z in range(groups):
        for s in range(spots):
            table[z, s] = 2 * (spots * (z % 2) + s) + z // 2
    return table


def host_tables(window, groups, spots):
    steps = window // groups
    gamma = ALPHA ** (1.0 / window)
    pairs = pair_numbers(window, groups, spots)
    cas = lambda k, n: np.cos(2 * np.pi * ((k * n) % window) / window) + np.sin(
        2 * np.pi * ((k * n) % window) / window
    )
    rows = np.arange(steps)
    merge = np.zeros((groups, 2, steps))
    split = np.zeros((groups, 2, steps))
    ahead = np.zeros((groups, spots, 2, 2, steps))
    back = np.zeros((groups, 2, steps, spots, 2))
    for z in range(groups):
        mine, other = steps * z + rows, steps * ((z + 2) % 4) + rows
        upper = z // 2
        merge[z, 0] = (-1.0 if upper else 1.0) * gamma**mine
        merge[z, 1] = gamma**other
        split[z, 0] = (-1.0 if upper else 1.0) * gamma**-mine / window
        split[z, 1] = gamma**-mine / window
        for s in range(spots):
            j = pairs[z, s]
            for f, k in enumerate((j, window // 2 if j == 0 else window - j)):
                for side, low in enumerate((z % 2, 1 - z % 2)):
                    ahead[z, s, f, side] = cas(k, steps * low + rows)
                    back[z, side, :, s, f] = cas(k, steps * low + rows)
    theta = 2 * np.pi * pairs / window
    plain = 1 - gamma * np.cos(theta)
    p_plus = np.where(pairs == 0, 1 - gamma, plain)
    p_minus = np.where(pairs == 0, 1 + gamma, plain)
    cross = np.where(pairs == 0, 0.0, gamma * np.sin(theta))
    scale = (np.sqrt(np.maximum(p_plus, p_minus) ** 2 + cross**2) * SIGMA_TOP + CURL_TOP) ** 2
    coef = np.stack([p_plus, p_minus, cross, 1 / scale], -1)
    center, radius = (UPPER + LOWER) / 2, (UPPER - LOWER) / 2
    now, cheb = radius / center, []
    for _ in range(SWEEPS - 1):
        later = 1.0 / (2.0 * center / radius - now)
        cheb += [later * now, 2.0 * later / radius]
        now = later
    flat = [np.asarray(v, np.float32).reshape(-1) for v in (merge, ahead, coef, cheb, back, split)]
    offsets = np.cumsum([0] + [v.size for v in flat]).tolist()
    table = np.zeros(-(-offsets[-1] // 1024) * 1024, np.float32)
    table[: offsets[-1]] = np.concatenate(flat)
    return table, offsets, 1 / center


class Part:
    def __init__(self, ref, offset):
        self.ref, self.offset = ref, offset

    def __getitem__(self, index):
        return self.ref[index + self.offset]


def window_kernel(
    steps, spots, offsets, inverse_center,
    conductance, table_hbm, force_hbm, start_hbm, region_hbm, iterate_hbm, out,
    table, force, start, region, latest, local_sem,
    got_last, got_far, mixed, got_near, extra, got_extra, mine_freq, spec, sigma,
    first, res, step, total, home, half, got_half, even, got_even,
    last_sem, far_sem, near_sem, extra_sem, sigma_sem, spec_sem, home_sem, half_sem, even_sem,
):
    z, s = lax.axis_index("tm"), lax.axis_index("space")
    far = ((z + 2) % 4, s)
    near = (z + 1 - 2 * (z % 2), s)
    peers = [(z, (s + hop) % spots) for hop in range(1, spots)]
    width = 6 // CHUNKS
    planes = 2 * spots
    parts = [pl.ds(c * width, width) for c in range(CHUNKS)]
    sent = []

    def send(source, target, sems, slot, device):
        copy = pltpu.make_async_remote_copy(
            src_ref=source, dst_ref=target,
            send_sem=sems.at[(0,) + slot], recv_sem=sems.at[(1,) + slot],
            device_id=device, device_id_type=pl.DeviceIdType.MESH,
        )
        copy.start()
        sent.append(copy)
        return copy

    barrier = pltpu.get_barrier_semaphore()
    for device in [far, near] + peers:
        pl.semaphore_signal(barrier, inc=1, device_id=device, device_id_type=pl.DeviceIdType.MESH)

    local = [
        pltpu.make_async_copy(source, target, local_sem.at[i])
        for i, (source, target) in enumerate([
            (region_hbm, region), (table_hbm, table), (force_hbm, force),
            (start_hbm, start), (iterate_hbm.at[steps - 1], latest),
        ])
    ]
    for copy in local:
        copy.start()
    merge, ahead, coef, cheb, back, split = [Part(table, offset) for offset in offsets[:-1]]
    local[0].wait()
    material = region[...]
    brick_sigma = jnp.zeros(material.shape, jnp.float32)
    for index in range(3):
        brick_sigma = brick_sigma + jnp.where(material == index, conductance[index], 0.0)
    sigma[s] = brick_sigma
    pl.semaphore_wait(barrier, 2 + len(peers))

    last_copy = pltpu.make_async_remote_copy(
        src_ref=iterate_hbm.at[steps - 1], dst_ref=got_last,
        send_sem=last_sem.at[0], recv_sem=last_sem.at[1],
        device_id=far, device_id_type=pl.DeviceIdType.MESH,
    )

    @pl.when(z == 3)
    def _():
        last_copy.start()

    far_copies = [
        send(force_hbm.at[:, part], got_far.at[:, part], far_sem, (c,), far)
        for c, part in enumerate(parts)
    ]
    sigma_copies = [
        send(sigma.at[s], sigma.at[s], sigma_sem, (h,), peer) for h, peer in enumerate(peers)
    ]
    for copy in local[1:]:
        copy.wait()
    extra[...] = jnp.zeros_like(extra)

    @pl.when(z == 1)
    def _():
        last_copy.wait_recv()
        extra[...] = got_last[...]

    @pl.when(z == 3)
    def _():
        last_copy.wait_send()
        extra[...] = latest[...]

    extra_copy = send(extra, got_extra, extra_sem, (0,), near)

    def mix(c):
        far_copies[c].wait_recv()

        def row(m, carry):
            w_mine, w_other = merge[z * 2 * steps + m], merge[(z * 2 + 1) * steps + m]
            for t in range(c * width, (c + 1) * width):
                mixed[m, t] = w_mine * force[m, t] + w_other * got_far[m, t]
            return carry

        lax.fori_loop(0, steps, row, 0, unroll=4)
        return send(mixed.at[:, parts[c]], got_near.at[:, parts[c]], near_sem, (c,), near)

    spec_copies = [None] * CHUNKS

    def transform(c, copy):
        copy.wait_recv()
        if c == 0:
            extra_copy.wait_recv()
            got_extra[...] = start[...] - ALPHA * (extra[...] + got_extra[...])
        jump = [brick_sigma[t % 2] * got_extra[t] for t in range(c * width, (c + 1) * width)]

        def slot(k, carry):
            base = (z * 2 * spots + k) * 2 * steps
            sums = [[j, None] for j in jump]
            for m in range(steps):
                w_mine, w_other = ahead[base + m], ahead[base + steps + m]
                for i in range(width):
                    t = c * width + i
                    term = w_other * got_near[m, t]
                    sums[i][0] = sums[i][0] + w_mine * mixed[m, t]
                    sums[i][1] = term if m == 0 else sums[i][1] + term
            for i in range(width):
                mine_freq[k // 2, c * width + i, k % 2] = sums[i][0] + sums[i][1]
            return carry

        lax.fori_loop(0, 2 * spots, slot, 0)
        spec[s, parts[c]] = mine_freq[s, parts[c]]
        spec_copies[c] = [
            send(mine_freq.at[peer[1], parts[c]], spec.at[s, parts[c]], spec_sem, (c, h), peer)
            for h, peer in enumerate(peers)
        ]

    pending = mix(0)
    for c in range(CHUNKS):
        later = mix(c + 1) if c + 1 < CHUNKS else None
        transform(c, pending)
        pending = later
    for copy in sigma_copies + [copy for group in spec_copies for copy in group]:
        copy.wait_recv()

    device = z * spots + s
    p_plus, p_minus = coef[device * 4], coef[device * 4 + 1]
    cross, inverse_scale = coef[device * 4 + 2], coef[device * 4 + 3]
    along_y = lax.broadcasted_iota(jnp.int32, (8, 128), 0)
    along_z = lax.broadcasted_iota(jnp.int32, (8, 128), 1)
    not_top_y, not_top_z = along_y < 7, along_z < 127
    not_low_y, not_low_z = along_y > 0, along_z > 0
    zero = jnp.zeros((8, 128), jnp.float32)

    def up_y(v):
        return jnp.where(not_top_y, pltpu.roll(v, 7, 0), 0.0)

    def up_z(v):
        return jnp.where(not_top_z, pltpu.roll(v, 127, 1), 0.0)

    def down_y(v):
        return jnp.where(not_low_y, pltpu.roll(v, 1, 0), 0.0)

    def down_z(v):
        return jnp.where(not_low_z, pltpu.roll(v, 1, 1), 0.0)

    def operator(buffer, sign, finish):
        load = lambda i: [[buffer[i // 2, 2 * e + i % 2, f] for e in range(3)] for f in range(2)]
        here = load(0)
        behind = [(zero, zero), (zero, zero)]
        for i in range(planes):
            ahead_field = load(i + 1) if i + 1 < planes else [[zero] * 3] * 2
            weight = sigma[i // 2, i % 2]
            weights = (weight * p_plus, weight * p_minus)
            weight_cross = weight * cross
            for f in range(2):
                ex, ey, ez = here[f]
                _, ey1, ez1 = ahead_field[f]
                bx = (up_y(ez) - ez) - (up_z(ey) - ey)
                by = (up_z(ex) - ex) - (ez1 - ez)
                bz = (ey1 - ey) - (up_y(ex) - ex)
                by0, bz0 = behind[f]
                curls = (
                    (down_z(by) - by) - (down_y(bz) - bz),
                    (bz0 - bz) - (down_z(bx) - bx),
                    (down_y(bx) - bx) - (by0 - by),
                )
                behind[f] = (by, bz)
                for e in range(3):
                    own = weights[f] * here[f][e]
                    swapped = weight_cross * here[1 - f][e]
                    value = curls[e] + own
                    value = value + swapped if (f == 1) == (sign > 0) else value - swapped
                    finish(i, e, f, value)
            here = ahead_field

    def begin(i, e, f, value):
        at = (i // 2, 2 * e + i % 2, f)
        res[at] = value
        step[at] = value * (inverse_scale * inverse_center)
        total[at] = zero

    operator(spec, -1.0, begin)

    def sweep(index, carry):
        w_step, w_res = cheb[index * 2], cheb[index * 2 + 1] * inverse_scale

        def keep(i, e, f, value):
            first[i // 2, 2 * e + i % 2, f] = value

        def advance(i, e, f, value):
            at = (i // 2, 2 * e + i % 2, f)
            old = step[at]
            total[at] = total[at] + old
            new = res[at] - value
            res[at] = new
            step[at] = w_step * old + w_res * new

        operator(step, 1.0, keep)
        operator(first, -1.0, advance)
        return carry

    lax.fori_loop(0, SWEEPS - 1, sweep, 0)

    home_copies = []
    for c, part in enumerate(parts):
        for b in range(spots):
            for t in range(c * width, (c + 1) * width):
                for f in range(2):
                    total[b, t, f] = total[b, t, f] + step[b, t, f]
        home[s, part] = total[s, part]
        home_copies.append([
            send(total.at[peer[1], part], home.at[s, part], home_sem, (c, h), peer)
            for h, peer in enumerate(peers)
        ])

    def gather(c):
        for copy in home_copies[c]:
            copy.wait_recv()

        def row(m, carry):
            base_mine = (z * 2 * steps + m) * 2 * spots
            base_other = ((z * 2 + 1) * steps + m) * 2 * spots
            for t in range(c * width, (c + 1) * width):
                mine, other = None, None
                for b in range(spots):
                    for f in range(2):
                        value = home[b, t, f]
                        term = back[base_mine + 2 * b + f] * value
                        mine = term if mine is None else mine + term
                        term = back[base_other + 2 * b + f] * value
                        other = term if other is None else other + term
                even[m, t] = mine
                half[m, t] = other
            return carry

        lax.fori_loop(0, steps, row, 0)
        return send(half.at[:, parts[c]], got_half.at[:, parts[c]], half_sem, (c,), near)

    def add(c, copy):
        copy.wait_recv()
        even[:, parts[c]] = even[:, parts[c]] + got_half[:, parts[c]]
        return send(even.at[:, parts[c]], got_even.at[:, parts[c]], even_sem, (c,), far)

    half_copies = [gather(0)]
    even_copies = []
    for c in range(CHUNKS):
        if c + 1 < CHUNKS:
            half_copies.append(gather(c + 1))
        even_copies.append(add(c, half_copies[c]))
    for c in range(CHUNKS):
        even_copies[c].wait_recv()

        def row(m, carry):
            w_mine, w_other = split[z * 2 * steps + m], split[(z * 2 + 1) * steps + m]
            for t in range(c * width, (c + 1) * width):
                out[m, t] = w_mine * even[m, t] + w_other * got_even[m, t]
            return carry

        lax.fori_loop(0, steps, row, 0, unroll=4)
    for copy in sent:
        copy.wait_send()


def pair_per_device(groups, spots, forcing, start_field, iterate, region, conductance):
    steps = forcing.shape[0]
    table, offsets, inverse_center = host_tables(steps * groups, groups, spots)
    tile = forcing.shape[3:]
    f32 = jnp.float32
    brick = lambda *lead: pltpu.VMEM(lead + tile, f32)
    rows = brick(steps, 6)
    grid = brick(spots, 6, 2)
    dma = pltpu.SemaphoreType.DMA
    smem, vmem = pl.BlockSpec(memory_space=pltpu.SMEM), pl.BlockSpec(memory_space=pltpu.VMEM)
    hbm = pl.BlockSpec(memory_space=pl.ANY)
    result = pl.pallas_call(
        functools.partial(window_kernel, steps, spots, offsets, inverse_center),
        out_shape=jax.ShapeDtypeStruct((steps, 6) + tile, f32),
        in_specs=[smem] + [hbm] * 5,
        out_specs=vmem,
        scratch_shapes=[
            pltpu.SMEM(table.shape, f32), rows, brick(6), pltpu.VMEM(region.shape, region.dtype),
            brick(6), dma((5,)),
            brick(6), rows, rows, rows, brick(6), brick(6), grid, grid, brick(spots, 2),
            grid, grid, grid, grid, grid, rows, rows, rows, rows,
            dma((2,)), dma((2, CHUNKS)), dma((2, CHUNKS)), dma((2, 1)), dma((2, spots - 1)),
            dma((2, CHUNKS, spots - 1)), dma((2, CHUNKS, spots - 1)),
            dma((2, CHUNKS)), dma((2, CHUNKS)),
        ],
        compiler_params=pltpu.CompilerParams(
            collective_id=0, has_side_effects=True, vmem_limit_bytes=32 * 1024 * 1024
        ),
    )(
        conductance, jnp.asarray(table),
        forcing.reshape((steps, 6) + tile), start_field.reshape((6,) + tile), region,
        iterate.reshape((steps, 6) + tile),
    )
    return result.reshape(forcing.shape)


def solution(mesh):
    placed = (
        P("tm", None, "space", None, None),
        P(None, "space", None, None),
        P("tm", None, "space", None, None),
        P("space", None, None),
        P(),
    )
    groups, spots = mesh.shape["tm"], mesh.shape["space"]

    def per_block(*arrays):
        steps, planes = arrays[0].shape[0], arrays[0].shape[2]
        one_each = steps * groups == 2 * groups * spots
        if groups == 4 and one_each and planes == 2 and arrays[0].shape[3:] == (8, 128):
            return pair_per_device(groups, spots, *arrays)
        return per_device(*arrays)

    return jax.shard_map(
        per_block,
        mesh=mesh,
        in_specs=placed,
        out_specs=P("tm", None, "space", None, None),
        check_vma=False,
    )
```

```python
import math

import functools

import jax
import jax.numpy as jnp
import numpy as np
from jax import lax
from jax.experimental import pallas as pl
from jax.experimental.pallas import tpu as pltpu
from jax.sharding import PartitionSpec as P

SWEEPS = 12


ALPHA = 0.1
LOWER = 0.02
UPPER = 1.0
SIGMA_TOP = 4.0
CURL_TOP = 12.0


def from_behind(value, axis, steps):
    count = lax.axis_size(axis)
    initial, last = (max(0, -steps), min(count, count - steps))
    return lax.ppermute(value, axis, [(source, source + steps) for source in range(initial, last)])


def broadcast(array, axis, root):
    mine = lax.axis_index(axis) == root
    return lax.psum(jnp.where(mine, array, jnp.zeros_like(array)), axis)


def forward_step(values, axis):
    inner = lax.slice_in_dim(values, 1, values.shape[axis], axis=axis)
    border = jnp.zeros_like(lax.slice_in_dim(values, 0, 1, axis=axis))
    return jnp.concatenate([inner, border], axis) - values


def backward_step(values, axis):
    inner = lax.slice_in_dim(values, 0, values.shape[axis] - 1, axis=axis)
    border = jnp.zeros_like(lax.slice_in_dim(values, 0, 1, axis=axis))
    return jnp.concatenate([border, inner], axis) - values


def curl_forward(field):
    field_x, field_y, field_z = (field[:, 0], field[:, 1], field[:, 2])
    lead_x, lead_y, lead_z = (field_x[:, :-1], field_y[:, :-1], field_z[:, :-1])
    flux_x = forward_step(lead_z, 2) - forward_step(lead_y, 3)
    flux_y = forward_step(lead_x, 3) - (field_z[:, 1:] - field_z[:, :-1])
    flux_z = field_y[:, 1:] - field_y[:, :-1] - forward_step(lead_x, 2)
    return jnp.stack([flux_x, flux_y, flux_z], axis=1)


def curl_adjoint(flux):
    flux_x, flux_y, flux_z = (flux[:, 0], flux[:, 1], flux[:, 2])
    tail_x, tail_y, tail_z = (flux_x[:, 1:], flux_y[:, 1:], flux_z[:, 1:])
    field_x = backward_step(tail_y, 3) - backward_step(tail_z, 2)
    field_y = flux_z[:, :-1] - flux_z[:, 1:] - backward_step(tail_x, 3)
    field_z = backward_step(tail_x, 2) - (flux_y[:, :-1] - flux_y[:, 1:])
    return jnp.stack([field_x, field_y, field_z], axis=1)


def brick_curl(field):
    upper = from_behind(field[:, :, :1], "space", -1)
    flux = curl_forward(jnp.concatenate([field, upper], 2))
    lower = from_behind(flux[:, :, -1:], "space", 1)
    return curl_adjoint(jnp.concatenate([lower, flux], 2))


def pair_terms(pairs, window):
    gamma = ALPHA ** (1.0 / window)
    angle = 2.0 * math.pi * pairs.astype(jnp.float32) / window
    plain = 1.0 - gamma * jnp.cos(angle)
    p_plus = jnp.where(pairs == 0, 1.0 - gamma, plain)
    p_minus = jnp.where(pairs == 0, 1.0 + gamma, plain)
    q_term = jnp.where(pairs == 0, 0.0, gamma * jnp.sin(angle))
    bound = jnp.sqrt(jnp.maximum(p_plus, p_minus) ** 2 + q_term**2) * SIGMA_TOP + CURL_TOP
    return (p_plus, p_minus, q_term, bound * bound)


def cas_table(freqs, window):
    moments = jnp.arange(window)
    product = freqs[:, None] * moments[None, :] % window
    angle = 2.0 * math.pi * product.astype(jnp.float32) / window
    return jnp.cos(angle) + jnp.sin(angle)


def powers(window, sign):
    gamma = jnp.float32(ALPHA ** (sign / window))
    return jnp.power(gamma, jnp.arange(window).astype(jnp.float32))


def frequency_order(window, steps):
    slots = jnp.arange(window)
    half = steps // 2
    within = slots % steps
    pairs = slots // steps * half + within % half
    mirror = jnp.where(pairs == 0, window // 2, window - pairs)
    return jnp.where(within < half, pairs, mirror)


def chebyshev_terms(count):
    center = (UPPER + LOWER) / 2.0
    radius = (UPPER - LOWER) / 2.0
    spread_ratio = center / radius
    weight_now = 1.0 / spread_ratio
    carry_terms, push_terms = ([], [])
    for _ in range(count):
        weight_next = 1.0 / (2.0 * spread_ratio - weight_now)
        carry_terms.append(weight_next * weight_now)
        push_terms.append(2.0 * weight_next / radius)
        weight_now = weight_next
    return (jnp.asarray(carry_terms, jnp.float32), jnp.asarray(push_terms, jnp.float32), center)


def per_device(forcing, start_field, iterate, region, conductance):
    steps = forcing.shape[0]
    half = steps // 2
    groups = lax.axis_size("tm")
    window = steps * groups
    depth_z = forcing.shape[4]
    sigma = jnp.zeros(region.shape, jnp.float32)
    for material in range(3):
        sigma = sigma + conductance[material] * (region == material).astype(jnp.float32)
    order = frequency_order(window, steps)
    forward_table = cas_table(order, window) * powers(window, 1.0)[None, :]
    inverse_table = cas_table(order, window).T * (powers(window, -1.0) / window)[:, None]
    flat = forcing.reshape(steps, groups, -1, depth_z)
    spread = jnp.einsum(
        "kn,ngrz->kgrz",
        forward_table,
        lax.all_to_all(flat, "tm", split_axis=1, concat_axis=0, tiled=True),
        precision=lax.Precision.HIGHEST,
    )
    spectrum = lax.all_to_all(spread, "tm", split_axis=0, concat_axis=1, tiled=True).reshape(
        forcing.shape
    )
    latest = broadcast(iterate[steps - 1], "tm", lax.axis_size("tm") - 1)
    spectrum = spectrum + (sigma * (start_field - ALPHA * latest))[None]
    pairs = lax.axis_index("tm") * half + jnp.arange(half)
    p_plus, p_minus, q_term, scale = pair_terms(pairs, window)
    diagonal_coef = jnp.concatenate([p_plus, p_minus]).reshape(steps, 1, 1, 1, 1)
    cross = q_term.reshape(half, 1, 1, 1, 1)
    norm_scale = jnp.concatenate([scale, scale]).reshape(steps, 1, 1, 1, 1)

    def couple(values, sign, weights):
        swapped = jnp.concatenate([-cross * values[half:], cross * values[:half]], 0)
        return weights * (diagonal_coef * values + sign * swapped)

    def normal(values):
        first = brick_curl(values) + couple(values, 1.0, sigma)
        return (brick_curl(first) + couple(first, -1.0, sigma)) / norm_scale

    start = (brick_curl(spectrum) + couple(spectrum, -1.0, sigma)) / norm_scale
    carry_terms, push_terms, center = chebyshev_terms(SWEEPS - 1)

    def sweep(sweep_index, carry_state):
        current, residual, direction = carry_state
        current = current + direction
        residual = residual - normal(direction)
        direction = carry_terms[sweep_index] * direction + push_terms[sweep_index] * residual
        return (current, residual, direction)

    current, residual, direction = lax.fori_loop(
        0, SWEEPS - 1, sweep, (jnp.zeros_like(start), start, start / center)
    )
    solution = (current + direction).reshape(steps, groups, -1, depth_z)
    spread_back = jnp.einsum(
        "nk,kgrz->ngrz",
        inverse_table,
        lax.all_to_all(solution, "tm", split_axis=1, concat_axis=0, tiled=True),
        precision=lax.Precision.HIGHEST,
    )
    updated = lax.all_to_all(spread_back, "tm", split_axis=0, concat_axis=1, tiled=True)
    return updated.reshape(forcing.shape)


VMEM_BYTES = 63 * 1024 * 1024
AHEAD = 2
CHUNKS = 6


def pair_numbers(window, groups, spots):
    table = np.zeros((groups, spots), np.int64)
    for z in range(groups):
        for s in range(spots):
            table[z, s] = 2 * (spots * (z % 2) + s) + z // 2
    return table


def host_tables(window, groups, spots):
    steps = window // groups
    gamma = ALPHA ** (1.0 / window)
    pairs = pair_numbers(window, groups, spots)
    cas = lambda k, n: np.cos(2 * np.pi * ((k * n) % window) / window) + np.sin(
        2 * np.pi * ((k * n) % window) / window
    )
    rows = np.arange(steps)
    merge = np.zeros((groups, 2, steps))
    split = np.zeros((groups, 2, steps))
    ahead = np.zeros((groups, spots, 2, 2, steps))
    back = np.zeros((groups, 2, steps, spots, 2))
    for z in range(groups):
        mine, other = steps * z + rows, steps * ((z + 2) % 4) + rows
        upper = z // 2
        merge[z, 0] = (-1.0 if upper else 1.0) * gamma**mine
        merge[z, 1] = gamma**other
        split[z, 0] = (-1.0 if upper else 1.0) * gamma**-mine / window
        split[z, 1] = gamma**-mine / window
        for s in range(spots):
            j = pairs[z, s]
            for f, k in enumerate((j, window // 2 if j == 0 else window - j)):
                for side, low in enumerate((z % 2, 1 - z % 2)):
                    ahead[z, s, f, side] = cas(k, steps * low + rows)
                    back[z, side, :, s, f] = cas(k, steps * low + rows)
    theta = 2 * np.pi * pairs / window
    plain = 1 - gamma * np.cos(theta)
    p_plus = np.where(pairs == 0, 1 - gamma, plain)
    p_minus = np.where(pairs == 0, 1 + gamma, plain)
    cross = np.where(pairs == 0, 0.0, gamma * np.sin(theta))
    scale = (np.sqrt(np.maximum(p_plus, p_minus) ** 2 + cross**2) * SIGMA_TOP + CURL_TOP) ** 2
    coef = np.stack([p_plus, p_minus, cross, 1 / scale], -1)
    center, radius = (UPPER + LOWER) / 2, (UPPER - LOWER) / 2
    now, cheb = radius / center, []
    for _ in range(SWEEPS - 1):
        later = 1.0 / (2.0 * center / radius - now)
        cheb += [later * now, 2.0 * later / radius]
        now = later
    flat = [np.asarray(v, np.float32).reshape(-1) for v in (merge, ahead, coef, cheb, back, split)]
    offsets = np.cumsum([0] + [v.size for v in flat]).tolist()
    table = np.zeros(-(-offsets[-1] // 1024) * 1024, np.float32)
    table[: offsets[-1]] = np.concatenate(flat)
    return table, offsets, 1 / center


class Part:
    def __init__(self, ref, offset):
        self.ref, self.offset = ref, offset

    def __getitem__(self, index):
        return self.ref[index + self.offset]


def window_kernel(
    steps, spots, offsets, inverse_center,
    conductance_hbm, table_hbm, force_hbm, start_hbm, region_hbm, iterate_hbm, out_hbm,
    out, out_sem, conductance, table, force, start, region, latest, local_sem,
    got_last, got_far, mixed, got_near, extra, got_extra, mine_freq, spec, sigma,
    first, res, step, total, home, half, got_half, even, got_even,
    last_sem, far_sem, near_sem, extra_sem, sigma_sem, spec_sem, home_sem, half_sem, even_sem,
):
    z, s = lax.axis_index("tm"), lax.axis_index("space")
    far = ((z + 2) % 4, s)
    near = (z + 1 - 2 * (z % 2), s)
    peers = [(z, (s + hop) % spots) for hop in range(1, spots)]
    width = 6 // CHUNKS
    planes = 2 * spots
    parts = [pl.ds(c * width, width) for c in range(CHUNKS)]
    sent = []

    def send(source, target, sems, slot, device):
        copy = pltpu.make_async_remote_copy(
            src_ref=source, dst_ref=target,
            send_sem=sems.at[(0,) + slot], recv_sem=sems.at[(1,) + slot],
            device_id=device, device_id_type=pl.DeviceIdType.MESH,
        )
        copy.start()
        sent.append(copy)
        return copy

    barrier = pltpu.get_barrier_semaphore()
    for device in [far, near] + peers:
        pl.semaphore_signal(barrier, inc=1, device_id=device, device_id_type=pl.DeviceIdType.MESH)

    local = [
        pltpu.make_async_copy(source, target, local_sem.at[i])
        for i, (source, target) in enumerate([
            (region_hbm, region), (conductance_hbm, conductance), (table_hbm, table), (force_hbm, force),
            (start_hbm, start), (iterate_hbm.at[steps - 1], latest),
        ])
    ]
    for copy in local:
        copy.start()
    merge, ahead, coef, cheb, back, split = [Part(table, offset) for offset in offsets[:-1]]
    local[0].wait()
    local[1].wait()
    material = region[...]
    brick_sigma = jnp.zeros(material.shape, jnp.float32)
    for index in range(3):
        brick_sigma = brick_sigma + jnp.where(material == index, conductance[index], 0.0)
    sigma[s] = brick_sigma
    pl.semaphore_wait(barrier, 2 + len(peers))

    last_copy = pltpu.make_async_remote_copy(
        src_ref=iterate_hbm.at[steps - 1], dst_ref=got_last,
        send_sem=last_sem.at[0], recv_sem=last_sem.at[1],
        device_id=far, device_id_type=pl.DeviceIdType.MESH,
    )

    @pl.when(z == 3)
    def _():
        last_copy.start()

    far_copies = []

    def send_far():
        c = len(far_copies)
        if c < CHUNKS:
            part = parts[c]
            far_copies.append(
                send(force_hbm.at[:, part], got_far.at[:, part], far_sem, (c,), far)
            )

    for _ in range(AHEAD):
        send_far()
    sigma_copies = [
        send(sigma.at[s], sigma.at[s], sigma_sem, (h,), peer) for h, peer in enumerate(peers)
    ]
    for copy in local[2:]:
        copy.wait()
    extra[...] = jnp.zeros_like(extra)

    @pl.when(z == 1)
    def _():
        last_copy.wait_recv()
        extra[...] = got_last[...]

    @pl.when(z == 3)
    def _():
        last_copy.wait_send()
        extra[...] = latest[...]

    extra_copy = send(extra, got_extra, extra_sem, (0,), near)

    def mix(c):
        far_copies[c].wait_recv()
        send_far()

        def row(m, carry):
            w_mine, w_other = merge[z * 2 * steps + m], merge[(z * 2 + 1) * steps + m]
            for t in range(c * width, (c + 1) * width):
                mixed[m, t] = w_mine * force[m, t] + w_other * got_far[m, t]
            return carry

        lax.fori_loop(0, steps, row, 0, unroll=4)
        return send(mixed.at[:, parts[c]], got_near.at[:, parts[c]], near_sem, (c,), near)

    spec_copies = [None] * CHUNKS

    def transform(c, copy):
        copy.wait_recv()
        if c == 0:
            extra_copy.wait_recv()
            got_extra[...] = start[...] - ALPHA * (extra[...] + got_extra[...])
        jump = [brick_sigma[t % 2] * got_extra[t] for t in range(c * width, (c + 1) * width)]

        def slot(k, carry):
            base = (z * 2 * spots + k) * 2 * steps
            sums = [[j, None] for j in jump]
            for m in range(steps):
                w_mine, w_other = ahead[base + m], ahead[base + steps + m]
                for i in range(width):
                    t = c * width + i
                    term = w_other * got_near[m, t]
                    sums[i][0] = sums[i][0] + w_mine * mixed[m, t]
                    sums[i][1] = term if m == 0 else sums[i][1] + term
            for i in range(width):
                mine_freq[k // 2, c * width + i, k % 2] = sums[i][0] + sums[i][1]
            return carry

        lax.fori_loop(0, 2 * spots, slot, 0)
        spec[s, parts[c]] = mine_freq[s, parts[c]]
        spec_copies[c] = [
            send(mine_freq.at[peer[1], parts[c]], spec.at[s, parts[c]], spec_sem, (c, h), peer)
            for h, peer in enumerate(peers)
        ]

    pending = mix(0)
    for c in range(CHUNKS):
        later = mix(c + 1) if c + 1 < CHUNKS else None
        transform(c, pending)
        pending = later
    for copy in sigma_copies + [copy for group in spec_copies for copy in group]:
        copy.wait_recv()

    device = z * spots + s
    p_plus, p_minus = coef[device * 4], coef[device * 4 + 1]
    cross, inverse_scale = coef[device * 4 + 2], coef[device * 4 + 3]
    along_y = lax.broadcasted_iota(jnp.int32, (8, 128), 0)
    along_z = lax.broadcasted_iota(jnp.int32, (8, 128), 1)
    not_top_y, not_top_z = along_y < 7, along_z < 127
    not_low_y, not_low_z = along_y > 0, along_z > 0
    zero = jnp.zeros((8, 128), jnp.float32)

    def up_y(v):
        return jnp.where(not_top_y, pltpu.roll(v, 7, 0), 0.0)

    def up_z(v):
        return jnp.where(not_top_z, pltpu.roll(v, 127, 1), 0.0)

    def down_y(v):
        return jnp.where(not_low_y, pltpu.roll(v, 1, 0), 0.0)

    def down_z(v):
        return jnp.where(not_low_z, pltpu.roll(v, 1, 1), 0.0)

    def operator(buffer, sign, finish):
        load = lambda i: [[buffer[i // 2, 2 * e + i % 2, f] for e in range(3)] for f in range(2)]
        here = load(0)
        behind = [(zero, zero), (zero, zero)]
        for i in range(planes):
            ahead_field = load(i + 1) if i + 1 < planes else [[zero] * 3] * 2
            weight = sigma[i // 2, i % 2]
            weights = (weight * p_plus, weight * p_minus)
            weight_cross = weight * cross
            for f in range(2):
                ex, ey, ez = here[f]
                _, ey1, ez1 = ahead_field[f]
                bx = (up_y(ez) - ez) - (up_z(ey) - ey)
                by = (up_z(ex) - ex) - (ez1 - ez)
                bz = (ey1 - ey) - (up_y(ex) - ex)
                by0, bz0 = behind[f]
                curls = (
                    (down_z(by) - by) - (down_y(bz) - bz),
                    (bz0 - bz) - (down_z(bx) - bx),
                    (down_y(bx) - bx) - (by0 - by),
                )
                behind[f] = (by, bz)
                for e in range(3):
                    own = weights[f] * here[f][e]
                    swapped = weight_cross * here[1 - f][e]
                    value = curls[e] + own
                    value = value + swapped if (f == 1) == (sign > 0) else value - swapped
                    finish(i, e, f, value)
            here = ahead_field

    def begin(i, e, f, value):
        at = (i // 2, 2 * e + i % 2, f)
        res[at] = value
        step[at] = value * (inverse_scale * inverse_center)
        total[at] = zero

    operator(spec, -1.0, begin)

    def sweep(index, carry):
        w_step, w_res = cheb[index * 2], cheb[index * 2 + 1] * inverse_scale

        def keep(i, e, f, value):
            first[i // 2, 2 * e + i % 2, f] = value

        def advance(i, e, f, value):
            at = (i // 2, 2 * e + i % 2, f)
            old = step[at]
            total[at] = total[at] + old
            new = res[at] - value
            res[at] = new
            step[at] = w_step * old + w_res * new

        operator(step, 1.0, keep)
        operator(first, -1.0, advance)
        return carry

    lax.fori_loop(0, SWEEPS - 1, sweep, 0)

    home_copies = []

    def send_home():
        c = len(home_copies)
        if c == CHUNKS:
            return
        part = parts[c]
        for b in range(spots):
            for t in range(c * width, (c + 1) * width):
                for f in range(2):
                    total[b, t, f] = total[b, t, f] + step[b, t, f]
        home[s, part] = total[s, part]
        home_copies.append([
            send(total.at[peer[1], part], home.at[s, part], home_sem, (c, h), peer)
            for h, peer in enumerate(peers)
        ])

    def gather(c):
        for copy in home_copies[c]:
            copy.wait_recv()

        def row(m, carry):
            base_mine = (z * 2 * steps + m) * 2 * spots
            base_other = ((z * 2 + 1) * steps + m) * 2 * spots
            for t in range(c * width, (c + 1) * width):
                mine, other = None, None
                for b in range(spots):
                    for f in range(2):
                        value = home[b, t, f]
                        term = back[base_mine + 2 * b + f] * value
                        mine = term if mine is None else mine + term
                        term = back[base_other + 2 * b + f] * value
                        other = term if other is None else other + term
                even[m, t] = mine
                half[m, t] = other
            return carry

        lax.fori_loop(0, steps, row, 0)
        return send(half.at[:, parts[c]], got_half.at[:, parts[c]], half_sem, (c,), near)

    def add(c, copy):
        copy.wait_recv()
        even[:, parts[c]] = even[:, parts[c]] + got_half[:, parts[c]]
        return send(even.at[:, parts[c]], got_even.at[:, parts[c]], even_sem, (c,), far)

    send_home()
    send_home()
    half_copies = [gather(0)]
    send_home()
    even_copies, out_copies = [], []
    for c in range(CHUNKS):
        if c + 1 < CHUNKS:
            half_copies.append(gather(c + 1))
            send_home()
        even_copies.append(add(c, half_copies[c]))
    for c in range(CHUNKS):
        even_copies[c].wait_recv()

        def row(m, carry):
            w_mine, w_other = split[z * 2 * steps + m], split[(z * 2 + 1) * steps + m]
            for t in range(c * width, (c + 1) * width):
                out[m, t] = w_mine * even[m, t] + w_other * got_even[m, t]
            return carry

        lax.fori_loop(0, steps, row, 0, unroll=4)
        out_copies.append(
            pltpu.make_async_copy(out.at[:, parts[c]], out_hbm.at[:, parts[c]], out_sem.at[c])
        )
        out_copies[c].start()
    for copy in sent:
        copy.wait_send()
    for copy in out_copies:
        copy.wait()


def pair_per_device(groups, spots, forcing, start_field, iterate, region, conductance):
    steps = forcing.shape[0]
    table, offsets, inverse_center = host_tables(steps * groups, groups, spots)
    tile = forcing.shape[3:]
    f32 = jnp.float32
    brick = lambda *lead: pltpu.VMEM(lead + tile, f32)
    rows = brick(steps, 6)
    grid = brick(spots, 6, 2)
    dma = pltpu.SemaphoreType.DMA
    hbm = pl.BlockSpec(memory_space=pl.ANY)
    result = pl.pallas_call(
        functools.partial(window_kernel, steps, spots, offsets, inverse_center),
        out_shape=jax.ShapeDtypeStruct((steps, 6) + tile, f32),
        in_specs=[hbm] * 6,
        out_specs=hbm,
        scratch_shapes=[
            rows, dma((CHUNKS,)), pltpu.SMEM(conductance.shape, f32), pltpu.SMEM(table.shape, f32), rows, brick(6), pltpu.VMEM(region.shape, region.dtype),
            brick(6), dma((6,)),
            brick(6), rows, rows, rows, brick(6), brick(6), grid, grid, brick(spots, 2),
            grid, grid, grid, grid, grid, rows, rows, rows, rows,
            dma((2,)), dma((2, CHUNKS)), dma((2, CHUNKS)), dma((2, 1)), dma((2, spots - 1)),
            dma((2, CHUNKS, spots - 1)), dma((2, CHUNKS, spots - 1)),
            dma((2, CHUNKS)), dma((2, CHUNKS)),
        ],
        compiler_params=pltpu.CompilerParams(
            collective_id=0, has_side_effects=True, vmem_limit_bytes=VMEM_BYTES
        ),
    )(
        conductance, jnp.asarray(table),
        forcing.reshape((steps, 6) + tile), start_field.reshape((6,) + tile), region,
        iterate.reshape((steps, 6) + tile),
    )
    return result.reshape(forcing.shape)


def solution(mesh):
    placed = (
        P("tm", None, "space", None, None),
        P(None, "space", None, None),
        P("tm", None, "space", None, None),
        P("space", None, None),
        P(),
    )
    groups, spots = mesh.shape["tm"], mesh.shape["space"]

    def per_block(*arrays):
        steps, planes = arrays[0].shape[0], arrays[0].shape[2]
        one_each = steps * groups == 2 * groups * spots
        if groups == 4 and one_each and planes == 2 and arrays[0].shape[3:] == (8, 128):
            return pair_per_device(groups, spots, *arrays)
        return per_device(*arrays)

    return jax.shard_map(
        per_block,
        mesh=mesh,
        in_specs=placed,
        out_specs=P("tm", None, "space", None, None),
        check_vma=False,
    )
```

```python
import math

import functools

import jax
import jax.numpy as jnp
import numpy as np
from jax import lax
from jax.experimental import pallas as pl
from jax.experimental.pallas import tpu as pltpu
from jax.sharding import PartitionSpec as P

SWEEPS = 12


ALPHA = 0.1
LOWER = 0.02
UPPER = 1.0
SIGMA_TOP = 4.0
CURL_TOP = 12.0


def from_behind(value, axis, steps):
    count = lax.axis_size(axis)
    initial, last = (max(0, -steps), min(count, count - steps))
    return lax.ppermute(value, axis, [(source, source + steps) for source in range(initial, last)])


def broadcast(array, axis, root):
    mine = lax.axis_index(axis) == root
    return lax.psum(jnp.where(mine, array, jnp.zeros_like(array)), axis)


def forward_step(values, axis):
    inner = lax.slice_in_dim(values, 1, values.shape[axis], axis=axis)
    border = jnp.zeros_like(lax.slice_in_dim(values, 0, 1, axis=axis))
    return jnp.concatenate([inner, border], axis) - values


def backward_step(values, axis):
    inner = lax.slice_in_dim(values, 0, values.shape[axis] - 1, axis=axis)
    border = jnp.zeros_like(lax.slice_in_dim(values, 0, 1, axis=axis))
    return jnp.concatenate([border, inner], axis) - values


def curl_forward(field):
    field_x, field_y, field_z = (field[:, 0], field[:, 1], field[:, 2])
    lead_x, lead_y, lead_z = (field_x[:, :-1], field_y[:, :-1], field_z[:, :-1])
    flux_x = forward_step(lead_z, 2) - forward_step(lead_y, 3)
    flux_y = forward_step(lead_x, 3) - (field_z[:, 1:] - field_z[:, :-1])
    flux_z = field_y[:, 1:] - field_y[:, :-1] - forward_step(lead_x, 2)
    return jnp.stack([flux_x, flux_y, flux_z], axis=1)


def curl_adjoint(flux):
    flux_x, flux_y, flux_z = (flux[:, 0], flux[:, 1], flux[:, 2])
    tail_x, tail_y, tail_z = (flux_x[:, 1:], flux_y[:, 1:], flux_z[:, 1:])
    field_x = backward_step(tail_y, 3) - backward_step(tail_z, 2)
    field_y = flux_z[:, :-1] - flux_z[:, 1:] - backward_step(tail_x, 3)
    field_z = backward_step(tail_x, 2) - (flux_y[:, :-1] - flux_y[:, 1:])
    return jnp.stack([field_x, field_y, field_z], axis=1)


def brick_curl(field):
    upper = from_behind(field[:, :, :1], "space", -1)
    flux = curl_forward(jnp.concatenate([field, upper], 2))
    lower = from_behind(flux[:, :, -1:], "space", 1)
    return curl_adjoint(jnp.concatenate([lower, flux], 2))


def pair_terms(pairs, window):
    gamma = ALPHA ** (1.0 / window)
    angle = 2.0 * math.pi * pairs.astype(jnp.float32) / window
    plain = 1.0 - gamma * jnp.cos(angle)
    p_plus = jnp.where(pairs == 0, 1.0 - gamma, plain)
    p_minus = jnp.where(pairs == 0, 1.0 + gamma, plain)
    q_term = jnp.where(pairs == 0, 0.0, gamma * jnp.sin(angle))
    bound = jnp.sqrt(jnp.maximum(p_plus, p_minus) ** 2 + q_term**2) * SIGMA_TOP + CURL_TOP
    return (p_plus, p_minus, q_term, bound * bound)


def cas_table(freqs, window):
    moments = jnp.arange(window)
    product = freqs[:, None] * moments[None, :] % window
    angle = 2.0 * math.pi * product.astype(jnp.float32) / window
    return jnp.cos(angle) + jnp.sin(angle)


def powers(window, sign):
    gamma = jnp.float32(ALPHA ** (sign / window))
    return jnp.power(gamma, jnp.arange(window).astype(jnp.float32))


def frequency_order(window, steps):
    slots = jnp.arange(window)
    half = steps // 2
    within = slots % steps
    pairs = slots // steps * half + within % half
    mirror = jnp.where(pairs == 0, window // 2, window - pairs)
    return jnp.where(within < half, pairs, mirror)


def chebyshev_terms(count):
    center = (UPPER + LOWER) / 2.0
    radius = (UPPER - LOWER) / 2.0
    spread_ratio = center / radius
    weight_now = 1.0 / spread_ratio
    carry_terms, push_terms = ([], [])
    for _ in range(count):
        weight_next = 1.0 / (2.0 * spread_ratio - weight_now)
        carry_terms.append(weight_next * weight_now)
        push_terms.append(2.0 * weight_next / radius)
        weight_now = weight_next
    return (jnp.asarray(carry_terms, jnp.float32), jnp.asarray(push_terms, jnp.float32), center)


def per_device(forcing, start_field, iterate, region, conductance):
    steps = forcing.shape[0]
    half = steps // 2
    groups = lax.axis_size("tm")
    window = steps * groups
    depth_z = forcing.shape[4]
    sigma = jnp.zeros(region.shape, jnp.float32)
    for material in range(3):
        sigma = sigma + conductance[material] * (region == material).astype(jnp.float32)
    order = frequency_order(window, steps)
    forward_table = cas_table(order, window) * powers(window, 1.0)[None, :]
    inverse_table = cas_table(order, window).T * (powers(window, -1.0) / window)[:, None]
    flat = forcing.reshape(steps, groups, -1, depth_z)
    spread = jnp.einsum(
        "kn,ngrz->kgrz",
        forward_table,
        lax.all_to_all(flat, "tm", split_axis=1, concat_axis=0, tiled=True),
        precision=lax.Precision.HIGHEST,
    )
    spectrum = lax.all_to_all(spread, "tm", split_axis=0, concat_axis=1, tiled=True).reshape(
        forcing.shape
    )
    latest = broadcast(iterate[steps - 1], "tm", lax.axis_size("tm") - 1)
    spectrum = spectrum + (sigma * (start_field - ALPHA * latest))[None]
    pairs = lax.axis_index("tm") * half + jnp.arange(half)
    p_plus, p_minus, q_term, scale = pair_terms(pairs, window)
    diagonal_coef = jnp.concatenate([p_plus, p_minus]).reshape(steps, 1, 1, 1, 1)
    cross = q_term.reshape(half, 1, 1, 1, 1)
    norm_scale = jnp.concatenate([scale, scale]).reshape(steps, 1, 1, 1, 1)

    def couple(values, sign, weights):
        swapped = jnp.concatenate([-cross * values[half:], cross * values[:half]], 0)
        return weights * (diagonal_coef * values + sign * swapped)

    def normal(values):
        first = brick_curl(values) + couple(values, 1.0, sigma)
        return (brick_curl(first) + couple(first, -1.0, sigma)) / norm_scale

    start = (brick_curl(spectrum) + couple(spectrum, -1.0, sigma)) / norm_scale
    carry_terms, push_terms, center = chebyshev_terms(SWEEPS - 1)

    def sweep(sweep_index, carry_state):
        current, residual, direction = carry_state
        current = current + direction
        residual = residual - normal(direction)
        direction = carry_terms[sweep_index] * direction + push_terms[sweep_index] * residual
        return (current, residual, direction)

    current, residual, direction = lax.fori_loop(
        0, SWEEPS - 1, sweep, (jnp.zeros_like(start), start, start / center)
    )
    solution = (current + direction).reshape(steps, groups, -1, depth_z)
    spread_back = jnp.einsum(
        "nk,kgrz->ngrz",
        inverse_table,
        lax.all_to_all(solution, "tm", split_axis=1, concat_axis=0, tiled=True),
        precision=lax.Precision.HIGHEST,
    )
    updated = lax.all_to_all(spread_back, "tm", split_axis=0, concat_axis=1, tiled=True)
    return updated.reshape(forcing.shape)


VMEM_BYTES = 63 * 1024 * 1024
AHEAD = 2
CHUNKS = 6


def pair_numbers(window, groups, spots):
    table = np.zeros((groups, spots), np.int64)
    for z in range(groups):
        for s in range(spots):
            table[z, s] = 2 * (spots * (z % 2) + s) + z // 2
    return table


def host_tables(window, groups, spots):
    steps = window // groups
    gamma = ALPHA ** (1.0 / window)
    pairs = pair_numbers(window, groups, spots)
    cas = lambda k, n: np.cos(2 * np.pi * ((k * n) % window) / window) + np.sin(
        2 * np.pi * ((k * n) % window) / window
    )
    rows = np.arange(steps)
    merge = np.zeros((groups, 2, steps))
    split = np.zeros((groups, 2, steps))
    ahead = np.zeros((groups, spots, 2, 2, steps))
    back = np.zeros((groups, 2, steps, spots, 2))
    for z in range(groups):
        mine, other = steps * z + rows, steps * ((z + 2) % 4) + rows
        upper = z // 2
        merge[z, 0] = (-1.0 if upper else 1.0) * gamma**mine
        merge[z, 1] = gamma**other
        split[z, 0] = (-1.0 if upper else 1.0) * gamma**-mine / window
        split[z, 1] = gamma**-mine / window
        for s in range(spots):
            j = pairs[z, s]
            for f, k in enumerate((j, window // 2 if j == 0 else window - j)):
                for side, low in enumerate((z % 2, 1 - z % 2)):
                    ahead[z, s, f, side] = cas(k, steps * low + rows)
                    back[z, side, :, s, f] = cas(k, steps * low + rows)
    theta = 2 * np.pi * pairs / window
    plain = 1 - gamma * np.cos(theta)
    p_plus = np.where(pairs == 0, 1 - gamma, plain)
    p_minus = np.where(pairs == 0, 1 + gamma, plain)
    cross = np.where(pairs == 0, 0.0, gamma * np.sin(theta))
    scale = (np.sqrt(np.maximum(p_plus, p_minus) ** 2 + cross**2) * SIGMA_TOP + CURL_TOP) ** 2
    coef = np.stack([p_plus, p_minus, cross, 1 / scale], -1)
    center, radius = (UPPER + LOWER) / 2, (UPPER - LOWER) / 2
    now, cheb = radius / center, []
    for _ in range(SWEEPS - 1):
        later = 1.0 / (2.0 * center / radius - now)
        cheb += [later * now, 2.0 * later / radius]
        now = later
    flat = [np.asarray(v, np.float32).reshape(-1) for v in (merge, ahead, coef, cheb, back, split)]
    offsets = np.cumsum([0] + [v.size for v in flat]).tolist()
    table = np.zeros(-(-offsets[-1] // 1024) * 1024, np.float32)
    table[: offsets[-1]] = np.concatenate(flat)
    return table, offsets, 1 / center


class Part:
    def __init__(self, ref, offset):
        self.ref, self.offset = ref, offset

    def __getitem__(self, index):
        return self.ref[index + self.offset]


def window_kernel(
    steps, spots, offsets, inverse_center,
    conductance_hbm, table_hbm, force_hbm, start_hbm, region_hbm, iterate_hbm, out_hbm,
    out, out_sem, conductance, table, force, start, region, latest, local_sem,
    got_last, got_far, mixed, got_near, extra, got_extra, mine_freq, spec, sigma,
    first, res, step, total, home, half, got_half, even, got_even,
    last_sem, far_sem, near_sem, extra_sem, sigma_sem, spec_sem, home_sem, half_sem, even_sem,
):
    z, s = lax.axis_index("tm"), lax.axis_index("space")
    far = ((z + 2) % 4, s)
    near = (z + 1 - 2 * (z % 2), s)
    peers = [(z, (s + hop) % spots) for hop in range(1, spots)]
    width = 6 // CHUNKS
    planes = 2 * spots
    parts = [pl.ds(c * width, width) for c in range(CHUNKS)]
    sent = []

    def send(source, target, sems, slot, device):
        copy = pltpu.make_async_remote_copy(
            src_ref=source, dst_ref=target,
            send_sem=sems.at[(0,) + slot], recv_sem=sems.at[(1,) + slot],
            device_id=device, device_id_type=pl.DeviceIdType.MESH,
        )
        copy.start()
        sent.append(copy)
        return copy

    barrier = pltpu.get_barrier_semaphore()
    for device in [far, near] + peers:
        pl.semaphore_signal(barrier, inc=1, device_id=device, device_id_type=pl.DeviceIdType.MESH)

    local = [
        pltpu.make_async_copy(source, target, local_sem.at[i])
        for i, (source, target) in enumerate([
            (region_hbm, region), (conductance_hbm, conductance), (table_hbm, table),
            (start_hbm, start), (iterate_hbm.at[steps - 1], latest),
            *[(force_hbm.at[:, i], force.at[i]) for i in range(6)],
        ])
    ]
    for copy in local:
        copy.start()
    merge, ahead, coef, cheb, back, split = [Part(table, offset) for offset in offsets[:-1]]
    local[0].wait()
    local[1].wait()
    material = region[...]
    brick_sigma = jnp.zeros(material.shape, jnp.float32)
    for index in range(3):
        brick_sigma = brick_sigma + jnp.where(material == index, conductance[index], 0.0)
    sigma[s] = brick_sigma
    pl.semaphore_wait(barrier, 2 + len(peers))

    last_copy = pltpu.make_async_remote_copy(
        src_ref=iterate_hbm.at[steps - 1], dst_ref=got_last,
        send_sem=last_sem.at[0], recv_sem=last_sem.at[1],
        device_id=far, device_id_type=pl.DeviceIdType.MESH,
    )

    @pl.when(z == 3)
    def _():
        last_copy.start()

    far_copies = []

    def send_far():
        c = len(far_copies)
        if c < CHUNKS:
            part = parts[c]
            for copy in local[5 + c * width : 5 + (c + 1) * width]:
                copy.wait()
            far_copies.append(send(force.at[part], got_far.at[part], far_sem, (c,), far))

    for _ in range(AHEAD):
        send_far()
    sigma_copies = [
        send(sigma.at[s], sigma.at[s], sigma_sem, (h,), peer) for h, peer in enumerate(peers)
    ]
    for copy in local[2:5]:
        copy.wait()
    extra[...] = jnp.zeros_like(extra)

    @pl.when(z == 1)
    def _():
        last_copy.wait_recv()
        extra[...] = got_last[...]

    @pl.when(z == 3)
    def _():
        last_copy.wait_send()
        extra[...] = latest[...]

    extra_copy = send(extra, got_extra, extra_sem, (0,), near)

    def mix(c):
        far_copies[c].wait_recv()
        send_far()

        def row(m, carry):
            w_mine, w_other = merge[z * 2 * steps + m], merge[(z * 2 + 1) * steps + m]
            for t in range(c * width, (c + 1) * width):
                mixed[t, m] = w_mine * force[t, m] + w_other * got_far[t, m]
            return carry

        lax.fori_loop(0, steps, row, 0, unroll=4)
        return send(mixed.at[parts[c]], got_near.at[parts[c]], near_sem, (c,), near)

    spec_copies = [None] * CHUNKS

    def transform(c, copy):
        copy.wait_recv()
        if c == 0:
            extra_copy.wait_recv()
            got_extra[...] = start[...] - ALPHA * (extra[...] + got_extra[...])
        jump = [brick_sigma[t % 2] * got_extra[t] for t in range(c * width, (c + 1) * width)]

        def slot(k, carry):
            base = (z * 2 * spots + k) * 2 * steps
            sums = [[j, None] for j in jump]
            for m in range(steps):
                w_mine, w_other = ahead[base + m], ahead[base + steps + m]
                for i in range(width):
                    t = c * width + i
                    term = w_other * got_near[t, m]
                    sums[i][0] = sums[i][0] + w_mine * mixed[t, m]
                    sums[i][1] = term if m == 0 else sums[i][1] + term
            for i in range(width):
                mine_freq[k // 2, c * width + i, k % 2] = sums[i][0] + sums[i][1]
            return carry

        lax.fori_loop(0, 2 * spots, slot, 0, unroll=4)
        spec[s, parts[c]] = mine_freq[s, parts[c]]
        spec_copies[c] = [
            send(mine_freq.at[peer[1], parts[c]], spec.at[s, parts[c]], spec_sem, (c, h), peer)
            for h, peer in enumerate(peers)
        ]

    pending = mix(0)
    for c in range(CHUNKS):
        later = mix(c + 1) if c + 1 < CHUNKS else None
        transform(c, pending)
        pending = later
    for copy in sigma_copies + [copy for group in spec_copies for copy in group]:
        copy.wait_recv()

    device = z * spots + s
    p_plus, p_minus = coef[device * 4], coef[device * 4 + 1]
    cross, inverse_scale = coef[device * 4 + 2], coef[device * 4 + 3]
    along_y = lax.broadcasted_iota(jnp.int32, (8, 128), 0)
    along_z = lax.broadcasted_iota(jnp.int32, (8, 128), 1)
    not_top_y, not_top_z = along_y < 7, along_z < 127
    not_low_y, not_low_z = along_y > 0, along_z > 0
    zero = jnp.zeros((8, 128), jnp.float32)

    def up_y(v):
        return jnp.where(not_top_y, pltpu.roll(v, 7, 0), 0.0)

    def up_z(v):
        return jnp.where(not_top_z, pltpu.roll(v, 127, 1), 0.0)

    def down_y(v):
        return jnp.where(not_low_y, pltpu.roll(v, 1, 0), 0.0)

    def down_z(v):
        return jnp.where(not_low_z, pltpu.roll(v, 1, 1), 0.0)

    def operator(buffer, sign, finish):
        load = lambda i: [[buffer[i // 2, 2 * e + i % 2, f] for e in range(3)] for f in range(2)]
        here = load(0)
        behind = [(zero, zero), (zero, zero)]
        for i in range(planes):
            ahead_field = load(i + 1) if i + 1 < planes else [[zero] * 3] * 2
            weight = sigma[i // 2, i % 2]
            weights = (weight * p_plus, weight * p_minus)
            weight_cross = weight * cross
            for f in range(2):
                ex, ey, ez = here[f]
                _, ey1, ez1 = ahead_field[f]
                bx = (up_y(ez) - ez) - (up_z(ey) - ey)
                by = (up_z(ex) - ex) - (ez1 - ez)
                bz = (ey1 - ey) - (up_y(ex) - ex)
                by0, bz0 = behind[f]
                curls = (
                    (down_z(by) - by) - (down_y(bz) - bz),
                    (bz0 - bz) - (down_z(bx) - bx),
                    (down_y(bx) - bx) - (by0 - by),
                )
                behind[f] = (by, bz)
                for e in range(3):
                    own = weights[f] * here[f][e]
                    swapped = weight_cross * here[1 - f][e]
                    value = curls[e] + own
                    value = value + swapped if (f == 1) == (sign > 0) else value - swapped
                    finish(i, e, f, value)
            here = ahead_field

    def begin(i, e, f, value):
        at = (i // 2, 2 * e + i % 2, f)
        res[at] = value
        step[at] = value * (inverse_scale * inverse_center)
        total[at] = zero

    operator(spec, -1.0, begin)

    def sweep(index, carry):
        w_step, w_res = cheb[index * 2], cheb[index * 2 + 1] * inverse_scale

        def keep(i, e, f, value):
            first[i // 2, 2 * e + i % 2, f] = value

        def advance(i, e, f, value):
            at = (i // 2, 2 * e + i % 2, f)
            old = step[at]
            total[at] = total[at] + old
            new = res[at] - value
            res[at] = new
            step[at] = w_step * old + w_res * new

        operator(step, 1.0, keep)
        operator(first, -1.0, advance)
        return carry

    lax.fori_loop(0, SWEEPS - 1, sweep, 0)

    home_copies = []

    def send_home():
        c = len(home_copies)
        if c == CHUNKS:
            return
        part = parts[c]
        for b in range(spots):
            for t in range(c * width, (c + 1) * width):
                for f in range(2):
                    total[b, t, f] = total[b, t, f] + step[b, t, f]
        home[s, part] = total[s, part]
        home_copies.append([
            send(total.at[peer[1], part], home.at[s, part], home_sem, (c, h), peer)
            for h, peer in enumerate(peers)
        ])

    def gather(c):
        for copy in home_copies[c]:
            copy.wait_recv()

        def row(m, carry):
            base_mine = (z * 2 * steps + m) * 2 * spots
            base_other = ((z * 2 + 1) * steps + m) * 2 * spots
            for t in range(c * width, (c + 1) * width):
                mine, other = [None, None], [None, None]
                for b in range(spots):
                    for f in range(2):
                        value = home[b, t, f]
                        term = back[base_mine + 2 * b + f] * value
                        mine[f] = term if b == 0 else mine[f] + term
                        term = back[base_other + 2 * b + f] * value
                        other[f] = term if b == 0 else other[f] + term
                even[t, m] = mine[0] + mine[1]
                half[t, m] = other[0] + other[1]
            return carry

        lax.fori_loop(0, steps, row, 0, unroll=4)
        return send(half.at[parts[c]], got_half.at[parts[c]], half_sem, (c,), near)

    def add(c, copy):
        copy.wait_recv()
        even[parts[c]] = even[parts[c]] + got_half[parts[c]]
        return send(even.at[parts[c]], got_even.at[parts[c]], even_sem, (c,), far)

    send_home()
    send_home()
    half_copies = [gather(0)]
    send_home()
    even_copies, out_copies = [], []
    for c in range(CHUNKS):
        if c + 1 < CHUNKS:
            half_copies.append(gather(c + 1))
            send_home()
        even_copies.append(add(c, half_copies[c]))
    for c in range(CHUNKS):
        even_copies[c].wait_recv()

        def row(m, carry):
            w_mine, w_other = split[z * 2 * steps + m], split[(z * 2 + 1) * steps + m]
            for t in range(c * width, (c + 1) * width):
                out[t, m] = w_mine * even[t, m] + w_other * got_even[t, m]
            return carry

        lax.fori_loop(0, steps, row, 0, unroll=4)
        for t in range(c * width, (c + 1) * width):
            out_copies.append(pltpu.make_async_copy(out.at[t], out_hbm.at[:, t], out_sem.at[t]))
            out_copies[t].start()
    for copy in sent:
        copy.wait_send()
    for copy in out_copies:
        copy.wait()


def pair_per_device(groups, spots, forcing, start_field, iterate, region, conductance):
    steps = forcing.shape[0]
    table, offsets, inverse_center = host_tables(steps * groups, groups, spots)
    tile = forcing.shape[3:]
    f32 = jnp.float32
    brick = lambda *lead: pltpu.VMEM(lead + tile, f32)
    rows = brick(6, steps)
    grid = brick(spots, 6, 2)
    dma = pltpu.SemaphoreType.DMA
    hbm = pl.BlockSpec(memory_space=pl.ANY)
    result = pl.pallas_call(
        functools.partial(window_kernel, steps, spots, offsets, inverse_center),
        out_shape=jax.ShapeDtypeStruct((steps, 6) + tile, f32),
        in_specs=[hbm] * 6,
        out_specs=hbm,
        scratch_shapes=[
            rows, dma((6,)), pltpu.SMEM(conductance.shape, f32), pltpu.SMEM(table.shape, f32), rows, brick(6), pltpu.VMEM(region.shape, region.dtype),
            brick(6), dma((11,)),
            brick(6), rows, rows, rows, brick(6), brick(6), grid, grid, brick(spots, 2),
            grid, grid, grid, grid, grid, rows, rows, rows, rows,
            dma((2,)), dma((2, CHUNKS)), dma((2, CHUNKS)), dma((2, 1)), dma((2, spots - 1)),
            dma((2, CHUNKS, spots - 1)), dma((2, CHUNKS, spots - 1)),
            dma((2, CHUNKS)), dma((2, CHUNKS)),
        ],
        compiler_params=pltpu.CompilerParams(
            collective_id=0, has_side_effects=True, vmem_limit_bytes=VMEM_BYTES
        ),
    )(
        conductance, jnp.asarray(table),
        forcing.reshape((steps, 6) + tile), start_field.reshape((6,) + tile), region,
        iterate.reshape((steps, 6) + tile),
    )
    return result.reshape(forcing.shape)


def solution(mesh):
    placed = (
        P("tm", None, "space", None, None),
        P(None, "space", None, None),
        P("tm", None, "space", None, None),
        P("space", None, None),
        P(),
    )
    groups, spots = mesh.shape["tm"], mesh.shape["space"]

    def per_block(*arrays):
        steps, planes = arrays[0].shape[0], arrays[0].shape[2]
        one_each = steps * groups == 2 * groups * spots
        if groups == 4 and one_each and planes == 2 and arrays[0].shape[3:] == (8, 128):
            return pair_per_device(groups, spots, *arrays)
        return per_device(*arrays)

    return jax.shard_map(
        per_block,
        mesh=mesh,
        in_specs=placed,
        out_specs=P("tm", None, "space", None, None),
        check_vma=False,
    )
```

```python
import math

import functools

import jax
import jax.numpy as jnp
import numpy as np
from jax import lax
from jax.experimental import pallas as pl
from jax.experimental.pallas import tpu as pltpu
from jax.sharding import PartitionSpec as P

SWEEPS = 12


ALPHA = 0.1
LOWER = 0.02
UPPER = 1.0
SIGMA_TOP = 4.0
CURL_TOP = 12.0


def from_behind(value, axis, steps):
    count = lax.axis_size(axis)
    initial, last = (max(0, -steps), min(count, count - steps))
    return lax.ppermute(value, axis, [(source, source + steps) for source in range(initial, last)])


def broadcast(array, axis, root):
    mine = lax.axis_index(axis) == root
    return lax.psum(jnp.where(mine, array, jnp.zeros_like(array)), axis)


def forward_step(values, axis):
    inner = lax.slice_in_dim(values, 1, values.shape[axis], axis=axis)
    border = jnp.zeros_like(lax.slice_in_dim(values, 0, 1, axis=axis))
    return jnp.concatenate([inner, border], axis) - values


def backward_step(values, axis):
    inner = lax.slice_in_dim(values, 0, values.shape[axis] - 1, axis=axis)
    border = jnp.zeros_like(lax.slice_in_dim(values, 0, 1, axis=axis))
    return jnp.concatenate([border, inner], axis) - values


def curl_forward(field):
    field_x, field_y, field_z = (field[:, 0], field[:, 1], field[:, 2])
    lead_x, lead_y, lead_z = (field_x[:, :-1], field_y[:, :-1], field_z[:, :-1])
    flux_x = forward_step(lead_z, 2) - forward_step(lead_y, 3)
    flux_y = forward_step(lead_x, 3) - (field_z[:, 1:] - field_z[:, :-1])
    flux_z = field_y[:, 1:] - field_y[:, :-1] - forward_step(lead_x, 2)
    return jnp.stack([flux_x, flux_y, flux_z], axis=1)


def curl_adjoint(flux):
    flux_x, flux_y, flux_z = (flux[:, 0], flux[:, 1], flux[:, 2])
    tail_x, tail_y, tail_z = (flux_x[:, 1:], flux_y[:, 1:], flux_z[:, 1:])
    field_x = backward_step(tail_y, 3) - backward_step(tail_z, 2)
    field_y = flux_z[:, :-1] - flux_z[:, 1:] - backward_step(tail_x, 3)
    field_z = backward_step(tail_x, 2) - (flux_y[:, :-1] - flux_y[:, 1:])
    return jnp.stack([field_x, field_y, field_z], axis=1)


def brick_curl(field):
    upper = from_behind(field[:, :, :1], "space", -1)
    flux = curl_forward(jnp.concatenate([field, upper], 2))
    lower = from_behind(flux[:, :, -1:], "space", 1)
    return curl_adjoint(jnp.concatenate([lower, flux], 2))


def pair_terms(pairs, window):
    gamma = ALPHA ** (1.0 / window)
    angle = 2.0 * math.pi * pairs.astype(jnp.float32) / window
    plain = 1.0 - gamma * jnp.cos(angle)
    p_plus = jnp.where(pairs == 0, 1.0 - gamma, plain)
    p_minus = jnp.where(pairs == 0, 1.0 + gamma, plain)
    q_term = jnp.where(pairs == 0, 0.0, gamma * jnp.sin(angle))
    bound = jnp.sqrt(jnp.maximum(p_plus, p_minus) ** 2 + q_term**2) * SIGMA_TOP + CURL_TOP
    return (p_plus, p_minus, q_term, bound * bound)


def cas_table(freqs, window):
    moments = jnp.arange(window)
    product = freqs[:, None] * moments[None, :] % window
    angle = 2.0 * math.pi * product.astype(jnp.float32) / window
    return jnp.cos(angle) + jnp.sin(angle)


def powers(window, sign):
    gamma = jnp.float32(ALPHA ** (sign / window))
    return jnp.power(gamma, jnp.arange(window).astype(jnp.float32))


def frequency_order(window, steps):
    slots = jnp.arange(window)
    half = steps // 2
    within = slots % steps
    pairs = slots // steps * half + within % half
    mirror = jnp.where(pairs == 0, window // 2, window - pairs)
    return jnp.where(within < half, pairs, mirror)


def chebyshev_terms(count):
    center = (UPPER + LOWER) / 2.0
    radius = (UPPER - LOWER) / 2.0
    spread_ratio = center / radius
    weight_now = 1.0 / spread_ratio
    carry_terms, push_terms = ([], [])
    for _ in range(count):
        weight_next = 1.0 / (2.0 * spread_ratio - weight_now)
        carry_terms.append(weight_next * weight_now)
        push_terms.append(2.0 * weight_next / radius)
        weight_now = weight_next
    return (jnp.asarray(carry_terms, jnp.float32), jnp.asarray(push_terms, jnp.float32), center)


def per_device(forcing, start_field, iterate, region, conductance):
    steps = forcing.shape[0]
    half = steps // 2
    groups = lax.axis_size("tm")
    window = steps * groups
    depth_z = forcing.shape[4]
    sigma = jnp.zeros(region.shape, jnp.float32)
    for material in range(3):
        sigma = sigma + conductance[material] * (region == material).astype(jnp.float32)
    order = frequency_order(window, steps)
    forward_table = cas_table(order, window) * powers(window, 1.0)[None, :]
    inverse_table = cas_table(order, window).T * (powers(window, -1.0) / window)[:, None]
    flat = forcing.reshape(steps, groups, -1, depth_z)
    spread = jnp.einsum(
        "kn,ngrz->kgrz",
        forward_table,
        lax.all_to_all(flat, "tm", split_axis=1, concat_axis=0, tiled=True),
        precision=lax.Precision.HIGHEST,
    )
    spectrum = lax.all_to_all(spread, "tm", split_axis=0, concat_axis=1, tiled=True).reshape(
        forcing.shape
    )
    latest = broadcast(iterate[steps - 1], "tm", lax.axis_size("tm") - 1)
    spectrum = spectrum + (sigma * (start_field - ALPHA * latest))[None]
    pairs = lax.axis_index("tm") * half + jnp.arange(half)
    p_plus, p_minus, q_term, scale = pair_terms(pairs, window)
    diagonal_coef = jnp.concatenate([p_plus, p_minus]).reshape(steps, 1, 1, 1, 1)
    cross = q_term.reshape(half, 1, 1, 1, 1)
    norm_scale = jnp.concatenate([scale, scale]).reshape(steps, 1, 1, 1, 1)

    def couple(values, sign, weights):
        swapped = jnp.concatenate([-cross * values[half:], cross * values[:half]], 0)
        return weights * (diagonal_coef * values + sign * swapped)

    def normal(values):
        first = brick_curl(values) + couple(values, 1.0, sigma)
        return (brick_curl(first) + couple(first, -1.0, sigma)) / norm_scale

    start = (brick_curl(spectrum) + couple(spectrum, -1.0, sigma)) / norm_scale
    carry_terms, push_terms, center = chebyshev_terms(SWEEPS - 1)

    def sweep(sweep_index, carry_state):
        current, residual, direction = carry_state
        current = current + direction
        residual = residual - normal(direction)
        direction = carry_terms[sweep_index] * direction + push_terms[sweep_index] * residual
        return (current, residual, direction)

    current, residual, direction = lax.fori_loop(
        0, SWEEPS - 1, sweep, (jnp.zeros_like(start), start, start / center)
    )
    solution = (current + direction).reshape(steps, groups, -1, depth_z)
    spread_back = jnp.einsum(
        "nk,kgrz->ngrz",
        inverse_table,
        lax.all_to_all(solution, "tm", split_axis=1, concat_axis=0, tiled=True),
        precision=lax.Precision.HIGHEST,
    )
    updated = lax.all_to_all(spread_back, "tm", split_axis=0, concat_axis=1, tiled=True)
    return updated.reshape(forcing.shape)


VMEM_BYTES = 63 * 1024 * 1024
AHEAD = 3
CHUNKS = 6


def pair_numbers(window, groups, spots):
    table = np.zeros((groups, spots), np.int64)
    for z in range(groups):
        for s in range(spots):
            table[z, s] = 2 * (spots * (z % 2) + s) + z // 2
    return table


def host_tables(window, groups, spots):
    steps = window // groups
    gamma = ALPHA ** (1.0 / window)
    pairs = pair_numbers(window, groups, spots)
    cas = lambda k, n: np.cos(2 * np.pi * ((k * n) % window) / window) + np.sin(
        2 * np.pi * ((k * n) % window) / window
    )
    rows = np.arange(steps)
    merge = np.zeros((groups, 2, steps))
    split = np.zeros((groups, 2, steps))
    ahead = np.zeros((groups, spots, 2, 2, steps))
    back = np.zeros((groups, 2, steps, spots, 2))
    for z in range(groups):
        mine, other = steps * z + rows, steps * ((z + 2) % 4) + rows
        upper = z // 2
        merge[z, 0] = (-1.0 if upper else 1.0) * gamma**mine
        merge[z, 1] = gamma**other
        split[z, 0] = (-1.0 if upper else 1.0) * gamma**-mine / window
        split[z, 1] = gamma**-mine / window
        for s in range(spots):
            j = pairs[z, s]
            for f, k in enumerate((j, window // 2 if j == 0 else window - j)):
                for side, low in enumerate((z % 2, 1 - z % 2)):
                    ahead[z, s, f, side] = cas(k, steps * low + rows)
                    back[z, side, :, s, f] = cas(k, steps * low + rows)
    theta = 2 * np.pi * pairs / window
    plain = 1 - gamma * np.cos(theta)
    p_plus = np.where(pairs == 0, 1 - gamma, plain)
    p_minus = np.where(pairs == 0, 1 + gamma, plain)
    cross = np.where(pairs == 0, 0.0, gamma * np.sin(theta))
    scale = (np.sqrt(np.maximum(p_plus, p_minus) ** 2 + cross**2) * SIGMA_TOP + CURL_TOP) ** 2
    coef = np.stack([p_plus, p_minus, cross, 1 / scale], -1)
    center, radius = (UPPER + LOWER) / 2, (UPPER - LOWER) / 2
    now, cheb = radius / center, []
    for _ in range(SWEEPS - 1):
        later = 1.0 / (2.0 * center / radius - now)
        cheb += [later * now, 2.0 * later / radius]
        now = later
    flat = [np.asarray(v, np.float32).reshape(-1) for v in (merge, ahead, coef, cheb, back, split)]
    offsets = np.cumsum([0] + [v.size for v in flat]).tolist()
    table = np.zeros(-(-offsets[-1] // 1024) * 1024, np.float32)
    table[: offsets[-1]] = np.concatenate(flat)
    return table, offsets, 1 / center


class Part:
    def __init__(self, ref, offset):
        self.ref, self.offset = ref, offset

    def __getitem__(self, index):
        return self.ref[index + self.offset]


def window_kernel(
    steps, spots, offsets, inverse_center,
    conductance_hbm, table_hbm, force_hbm, start_hbm, region_hbm, iterate_hbm, out_hbm,
    out, out_sem, conductance, table, force, start, region, latest, local_sem,
    got_last, got_far, mixed, got_near, extra, got_extra, mine_freq, spec, sigma,
    res, step, total, home, half, got_half, even, got_even,
    last_sem, far_sem, near_sem, extra_sem, sigma_sem, spec_sem, home_sem, half_sem, even_sem,
):
    z, s = lax.axis_index("tm"), lax.axis_index("space")
    far = ((z + 2) % 4, s)
    near = (z + 1 - 2 * (z % 2), s)
    peers = [(z, (s + hop) % spots) for hop in range(1, spots)]
    width = 6 // CHUNKS
    planes = 2 * spots
    parts = [pl.ds(c * width, width) for c in range(CHUNKS)]
    sent = []

    def send(source, target, sems, slot, device):
        copy = pltpu.make_async_remote_copy(
            src_ref=source, dst_ref=target,
            send_sem=sems.at[(0,) + slot], recv_sem=sems.at[(1,) + slot],
            device_id=device, device_id_type=pl.DeviceIdType.MESH,
        )
        copy.start()
        sent.append(copy)
        return copy

    barrier = pltpu.get_barrier_semaphore()
    for device in [far, near] + peers:
        pl.semaphore_signal(barrier, inc=1, device_id=device, device_id_type=pl.DeviceIdType.MESH)

    local = [
        pltpu.make_async_copy(source, target, local_sem.at[i])
        for i, (source, target) in enumerate([
            (region_hbm, region), (conductance_hbm, conductance), (table_hbm, table),
            (start_hbm, start), (iterate_hbm.at[steps - 1], latest),
            *[(force_hbm.at[:, i], force.at[i]) for i in range(6)],
        ])
    ]
    for copy in local:
        copy.start()
    merge, ahead, coef, cheb, back, split = [Part(table, offset) for offset in offsets[:-1]]
    local[0].wait()
    local[1].wait()
    material = region[...]
    brick_sigma = jnp.zeros(material.shape, jnp.float32)
    for index in range(3):
        brick_sigma = brick_sigma + jnp.where(material == index, conductance[index], 0.0)
    sigma[s] = brick_sigma
    pl.semaphore_wait(barrier, 2 + len(peers))

    last_copy = pltpu.make_async_remote_copy(
        src_ref=iterate_hbm.at[steps - 1], dst_ref=got_last,
        send_sem=last_sem.at[0], recv_sem=last_sem.at[1],
        device_id=far, device_id_type=pl.DeviceIdType.MESH,
    )

    @pl.when(z == 3)
    def _():
        last_copy.start()

    far_copies = []

    def send_far():
        c = len(far_copies)
        if c < CHUNKS:
            part = parts[c]
            for copy in local[5 + c * width : 5 + (c + 1) * width]:
                copy.wait()
            far_copies.append(send(force.at[part], got_far.at[part], far_sem, (c,), far))

    for _ in range(AHEAD):
        send_far()
    sigma_copies = [
        send(sigma.at[s], sigma.at[s], sigma_sem, (h,), peer) for h, peer in enumerate(peers)
    ]
    for copy in local[2:5]:
        copy.wait()
    extra[...] = jnp.zeros_like(extra)

    @pl.when(z == 1)
    def _():
        last_copy.wait_recv()
        extra[...] = got_last[...]

    @pl.when(z == 3)
    def _():
        last_copy.wait_send()
        extra[...] = latest[...]

    extra_copy = send(extra, got_extra, extra_sem, (0,), near)

    def mix(c):
        far_copies[c].wait_recv()
        send_far()

        def row(m, carry):
            w_mine, w_other = merge[z * 2 * steps + m], merge[(z * 2 + 1) * steps + m]
            for t in range(c * width, (c + 1) * width):
                mixed[t, m] = w_mine * force[t, m] + w_other * got_far[t, m]
            return carry

        lax.fori_loop(0, steps, row, 0, unroll=4)
        return send(mixed.at[parts[c]], got_near.at[parts[c]], near_sem, (c,), near)

    spec_copies = [None] * CHUNKS

    def transform(c, copy):
        copy.wait_recv()
        if c == 0:
            extra_copy.wait_recv()
            got_extra[...] = start[...] - ALPHA * (extra[...] + got_extra[...])
        jump = [brick_sigma[t % 2] * got_extra[t] for t in range(c * width, (c + 1) * width)]

        def slot(k, carry):
            base = (z * 2 * spots + k) * 2 * steps
            sums = [[j, None] for j in jump]
            for m in range(steps):
                w_mine, w_other = ahead[base + m], ahead[base + steps + m]
                for i in range(width):
                    t = c * width + i
                    term = w_other * got_near[t, m]
                    sums[i][0] = sums[i][0] + w_mine * mixed[t, m]
                    sums[i][1] = term if m == 0 else sums[i][1] + term
            for i in range(width):
                mine_freq[k // 2, c * width + i, k % 2] = sums[i][0] + sums[i][1]
            return carry

        lax.fori_loop(0, 2 * spots, slot, 0, unroll=4)
        spec[s, parts[c]] = mine_freq[s, parts[c]]
        spec_copies[c] = [
            send(mine_freq.at[peer[1], parts[c]], spec.at[s, parts[c]], spec_sem, (c, h), peer)
            for h, peer in enumerate(peers)
        ]

    pending = mix(0)
    for c in range(CHUNKS):
        later = mix(c + 1) if c + 1 < CHUNKS else None
        transform(c, pending)
        pending = later
    for copy in sigma_copies + [copy for group in spec_copies for copy in group]:
        copy.wait_recv()

    device = z * spots + s
    p_plus, p_minus = coef[device * 4], coef[device * 4 + 1]
    cross, inverse_scale = coef[device * 4 + 2], coef[device * 4 + 3]
    along_y = lax.broadcasted_iota(jnp.int32, (8, 128), 0)
    along_z = lax.broadcasted_iota(jnp.int32, (8, 128), 1)
    not_top_y, not_top_z = along_y < 7, along_z < 127
    not_low_y, not_low_z = along_y > 0, along_z > 0
    zero = jnp.zeros((8, 128), jnp.float32)

    def up_y(v):
        return jnp.where(not_top_y, pltpu.roll(v, 7, 0), 0.0)

    def up_z(v):
        return jnp.where(not_top_z, pltpu.roll(v, 127, 1), 0.0)

    def down_y(v):
        return jnp.where(not_low_y, pltpu.roll(v, 1, 0), 0.0)

    def down_z(v):
        return jnp.where(not_low_z, pltpu.roll(v, 1, 1), 0.0)

    def planes_of(buffer):
        return lambda i: [
            [buffer[i // 2, 2 * e + i % 2, f] for e in range(3)] for f in range(2)
        ]

    def operator(load, sign, finish):
        here = load(0)
        behind = [(zero, zero), (zero, zero)]
        for i in range(planes):
            ahead_field = load(i + 1) if i + 1 < planes else [[zero] * 3] * 2
            weight = sigma[i // 2, i % 2]
            weights = (weight * p_plus, weight * p_minus)
            weight_cross = weight * cross
            for f in range(2):
                ex, ey, ez = here[f]
                _, ey1, ez1 = ahead_field[f]
                bx = (up_y(ez) - ez) - (up_z(ey) - ey)
                by = (up_z(ex) - ex) - (ez1 - ez)
                bz = (ey1 - ey) - (up_y(ex) - ex)
                by0, bz0 = behind[f]
                curls = (
                    (down_z(by) - by) - (down_y(bz) - bz),
                    (bz0 - bz) - (down_z(bx) - bx),
                    (down_y(bx) - bx) - (by0 - by),
                )
                behind[f] = (by, bz)
                for e in range(3):
                    own = weights[f] * here[f][e]
                    swapped = weight_cross * here[1 - f][e]
                    value = curls[e] + own
                    value = value + swapped if (f == 1) == (sign > 0) else value - swapped
                    finish(i, e, f, value)
            here = ahead_field
            yield

    def begin(i, e, f, value):
        at = (i // 2, 2 * e + i % 2, f)
        res[at] = value
        step[at] = value * (inverse_scale * inverse_center)
        total[at] = zero

    for _ in operator(planes_of(spec), -1.0, begin):
        pass

    def sweep(index, carry):
        w_step, w_res = cheb[index * 2], cheb[index * 2 + 1] * inverse_scale

        first = [[[None] * 3 for _ in range(2)] for _ in range(planes)]

        def keep(i, e, f, value):
            first[i][f][e] = value

        def advance(i, e, f, value):
            at = (i // 2, 2 * e + i % 2, f)
            old = step[at]
            total[at] = total[at] + old
            new = res[at] - value
            res[at] = new
            step[at] = w_step * old + w_res * new

        ahead_pass = operator(planes_of(step), 1.0, keep)
        behind_pass = operator(lambda i: first[i], -1.0, advance)
        next(ahead_pass)
        for _ in range(planes - 1):
            next(ahead_pass)
            next(behind_pass)
        next(behind_pass)
        return carry

    lax.fori_loop(0, SWEEPS - 1, sweep, 0)

    home_copies = []

    def send_home():
        c = len(home_copies)
        if c == CHUNKS:
            return
        part = parts[c]
        for b in range(spots):
            for t in range(c * width, (c + 1) * width):
                for f in range(2):
                    total[b, t, f] = total[b, t, f] + step[b, t, f]
        home[s, part] = total[s, part]
        home_copies.append([
            send(total.at[peer[1], part], home.at[s, part], home_sem, (c, h), peer)
            for h, peer in enumerate(peers)
        ])

    def gather(c):
        for copy in home_copies[c]:
            copy.wait_recv()

        def row(m, carry):
            base_mine = (z * 2 * steps + m) * 2 * spots
            base_other = ((z * 2 + 1) * steps + m) * 2 * spots
            for t in range(c * width, (c + 1) * width):
                mine, other = [None, None], [None, None]
                for b in range(spots):
                    for f in range(2):
                        value = home[b, t, f]
                        term = back[base_mine + 2 * b + f] * value
                        mine[f] = term if b == 0 else mine[f] + term
                        term = back[base_other + 2 * b + f] * value
                        other[f] = term if b == 0 else other[f] + term
                even[t, m] = mine[0] + mine[1]
                half[t, m] = other[0] + other[1]
            return carry

        lax.fori_loop(0, steps, row, 0, unroll=4)
        return send(half.at[parts[c]], got_half.at[parts[c]], half_sem, (c,), near)

    def add(c, copy):
        copy.wait_recv()
        even[parts[c]] = even[parts[c]] + got_half[parts[c]]
        return send(even.at[parts[c]], got_even.at[parts[c]], even_sem, (c,), far)

    send_home()
    send_home()
    half_copies = [gather(0)]
    send_home()
    even_copies, out_copies = [], []
    for c in range(CHUNKS):
        if c + 1 < CHUNKS:
            half_copies.append(gather(c + 1))
            send_home()
        even_copies.append(add(c, half_copies[c]))
    for c in range(CHUNKS):
        even_copies[c].wait_recv()

        def row(m, carry):
            w_mine, w_other = split[z * 2 * steps + m], split[(z * 2 + 1) * steps + m]
            for t in range(c * width, (c + 1) * width):
                out[t, m] = w_mine * even[t, m] + w_other * got_even[t, m]
            return carry

        lax.fori_loop(0, steps, row, 0, unroll=4)
        for t in range(c * width, (c + 1) * width):
            out_copies.append(pltpu.make_async_copy(out.at[t], out_hbm.at[:, t], out_sem.at[t]))
            out_copies[t].start()
    for copy in sent:
        copy.wait_send()
    for copy in out_copies:
        copy.wait()


def pair_per_device(groups, spots, forcing, start_field, iterate, region, conductance):
    steps = forcing.shape[0]
    table, offsets, inverse_center = host_tables(steps * groups, groups, spots)
    tile = forcing.shape[3:]
    f32 = jnp.float32
    brick = lambda *lead: pltpu.VMEM(lead + tile, f32)
    rows = brick(6, steps)
    grid = brick(spots, 6, 2)
    dma = pltpu.SemaphoreType.DMA
    hbm = pl.BlockSpec(memory_space=pl.ANY)
    result = pl.pallas_call(
        functools.partial(window_kernel, steps, spots, offsets, inverse_center),
        out_shape=jax.ShapeDtypeStruct((steps, 6) + tile, f32),
        in_specs=[hbm] * 6,
        out_specs=hbm,
        scratch_shapes=[
            rows, dma((6,)), pltpu.SMEM(conductance.shape, f32), pltpu.SMEM(table.shape, f32), rows, brick(6), pltpu.VMEM(region.shape, region.dtype),
            brick(6), dma((11,)),
            brick(6), rows, rows, rows, brick(6), brick(6), grid, grid, brick(spots, 2),
            grid, grid, grid, grid, rows, rows, rows, rows,
            dma((2,)), dma((2, CHUNKS)), dma((2, CHUNKS)), dma((2, 1)), dma((2, spots - 1)),
            dma((2, CHUNKS, spots - 1)), dma((2, CHUNKS, spots - 1)),
            dma((2, CHUNKS)), dma((2, CHUNKS)),
        ],
        compiler_params=pltpu.CompilerParams(
            collective_id=0, has_side_effects=True, vmem_limit_bytes=VMEM_BYTES
        ),
    )(
        conductance, jnp.asarray(table),
        forcing.reshape((steps, 6) + tile), start_field.reshape((6,) + tile), region,
        iterate.reshape((steps, 6) + tile),
    )
    return result.reshape(forcing.shape)


def solution(mesh):
    placed = (
        P("tm", None, "space", None, None),
        P(None, "space", None, None),
        P("tm", None, "space", None, None),
        P("space", None, None),
        P(),
    )
    groups, spots = mesh.shape["tm"], mesh.shape["space"]

    def per_block(*arrays):
        steps, planes = arrays[0].shape[0], arrays[0].shape[2]
        one_each = steps * groups == 2 * groups * spots
        if groups == 4 and one_each and planes == 2 and arrays[0].shape[3:] == (8, 128):
            return pair_per_device(groups, spots, *arrays)
        return per_device(*arrays)

    return jax.shard_map(
        per_block,
        mesh=mesh,
        in_specs=placed,
        out_specs=P("tm", None, "space", None, None),
        check_vma=False,
    )
```

```python
import math

import functools

import jax
import jax.numpy as jnp
import numpy as np
from jax import lax
from jax.experimental import pallas as pl
from jax.experimental.pallas import tpu as pltpu
from jax.sharding import PartitionSpec as P

SWEEPS = 12


ALPHA = 0.1
LOWER = 0.02
UPPER = 1.0
SIGMA_TOP = 4.0
CURL_TOP = 12.0


def from_behind(value, axis, steps):
    count = lax.axis_size(axis)
    initial, last = (max(0, -steps), min(count, count - steps))
    return lax.ppermute(value, axis, [(source, source + steps) for source in range(initial, last)])


def broadcast(array, axis, root):
    mine = lax.axis_index(axis) == root
    return lax.psum(jnp.where(mine, array, jnp.zeros_like(array)), axis)


def forward_step(values, axis):
    inner = lax.slice_in_dim(values, 1, values.shape[axis], axis=axis)
    border = jnp.zeros_like(lax.slice_in_dim(values, 0, 1, axis=axis))
    return jnp.concatenate([inner, border], axis) - values


def backward_step(values, axis):
    inner = lax.slice_in_dim(values, 0, values.shape[axis] - 1, axis=axis)
    border = jnp.zeros_like(lax.slice_in_dim(values, 0, 1, axis=axis))
    return jnp.concatenate([border, inner], axis) - values


def curl_forward(field):
    field_x, field_y, field_z = (field[:, 0], field[:, 1], field[:, 2])
    lead_x, lead_y, lead_z = (field_x[:, :-1], field_y[:, :-1], field_z[:, :-1])
    flux_x = forward_step(lead_z, 2) - forward_step(lead_y, 3)
    flux_y = forward_step(lead_x, 3) - (field_z[:, 1:] - field_z[:, :-1])
    flux_z = field_y[:, 1:] - field_y[:, :-1] - forward_step(lead_x, 2)
    return jnp.stack([flux_x, flux_y, flux_z], axis=1)


def curl_adjoint(flux):
    flux_x, flux_y, flux_z = (flux[:, 0], flux[:, 1], flux[:, 2])
    tail_x, tail_y, tail_z = (flux_x[:, 1:], flux_y[:, 1:], flux_z[:, 1:])
    field_x = backward_step(tail_y, 3) - backward_step(tail_z, 2)
    field_y = flux_z[:, :-1] - flux_z[:, 1:] - backward_step(tail_x, 3)
    field_z = backward_step(tail_x, 2) - (flux_y[:, :-1] - flux_y[:, 1:])
    return jnp.stack([field_x, field_y, field_z], axis=1)


def brick_curl(field):
    upper = from_behind(field[:, :, :1], "space", -1)
    flux = curl_forward(jnp.concatenate([field, upper], 2))
    lower = from_behind(flux[:, :, -1:], "space", 1)
    return curl_adjoint(jnp.concatenate([lower, flux], 2))


def pair_terms(pairs, window):
    gamma = ALPHA ** (1.0 / window)
    angle = 2.0 * math.pi * pairs.astype(jnp.float32) / window
    plain = 1.0 - gamma * jnp.cos(angle)
    p_plus = jnp.where(pairs == 0, 1.0 - gamma, plain)
    p_minus = jnp.where(pairs == 0, 1.0 + gamma, plain)
    q_term = jnp.where(pairs == 0, 0.0, gamma * jnp.sin(angle))
    bound = jnp.sqrt(jnp.maximum(p_plus, p_minus) ** 2 + q_term**2) * SIGMA_TOP + CURL_TOP
    return (p_plus, p_minus, q_term, bound * bound)


def cas_table(freqs, window):
    moments = jnp.arange(window)
    product = freqs[:, None] * moments[None, :] % window
    angle = 2.0 * math.pi * product.astype(jnp.float32) / window
    return jnp.cos(angle) + jnp.sin(angle)


def powers(window, sign):
    gamma = jnp.float32(ALPHA ** (sign / window))
    return jnp.power(gamma, jnp.arange(window).astype(jnp.float32))


def frequency_order(window, steps):
    slots = jnp.arange(window)
    half = steps // 2
    within = slots % steps
    pairs = slots // steps * half + within % half
    mirror = jnp.where(pairs == 0, window // 2, window - pairs)
    return jnp.where(within < half, pairs, mirror)


def chebyshev_terms(count):
    center = (UPPER + LOWER) / 2.0
    radius = (UPPER - LOWER) / 2.0
    spread_ratio = center / radius
    weight_now = 1.0 / spread_ratio
    carry_terms, push_terms = ([], [])
    for _ in range(count):
        weight_next = 1.0 / (2.0 * spread_ratio - weight_now)
        carry_terms.append(weight_next * weight_now)
        push_terms.append(2.0 * weight_next / radius)
        weight_now = weight_next
    return (jnp.asarray(carry_terms, jnp.float32), jnp.asarray(push_terms, jnp.float32), center)


def per_device(forcing, start_field, iterate, region, conductance):
    steps = forcing.shape[0]
    half = steps // 2
    groups = lax.axis_size("tm")
    window = steps * groups
    depth_z = forcing.shape[4]
    sigma = jnp.zeros(region.shape, jnp.float32)
    for material in range(3):
        sigma = sigma + conductance[material] * (region == material).astype(jnp.float32)
    order = frequency_order(window, steps)
    forward_table = cas_table(order, window) * powers(window, 1.0)[None, :]
    inverse_table = cas_table(order, window).T * (powers(window, -1.0) / window)[:, None]
    flat = forcing.reshape(steps, groups, -1, depth_z)
    spread = jnp.einsum(
        "kn,ngrz->kgrz",
        forward_table,
        lax.all_to_all(flat, "tm", split_axis=1, concat_axis=0, tiled=True),
        precision=lax.Precision.HIGHEST,
    )
    spectrum = lax.all_to_all(spread, "tm", split_axis=0, concat_axis=1, tiled=True).reshape(
        forcing.shape
    )
    latest = broadcast(iterate[steps - 1], "tm", lax.axis_size("tm") - 1)
    spectrum = spectrum + (sigma * (start_field - ALPHA * latest))[None]
    pairs = lax.axis_index("tm") * half + jnp.arange(half)
    p_plus, p_minus, q_term, scale = pair_terms(pairs, window)
    diagonal_coef = jnp.concatenate([p_plus, p_minus]).reshape(steps, 1, 1, 1, 1)
    cross = q_term.reshape(half, 1, 1, 1, 1)
    norm_scale = jnp.concatenate([scale, scale]).reshape(steps, 1, 1, 1, 1)

    def couple(values, sign, weights):
        swapped = jnp.concatenate([-cross * values[half:], cross * values[:half]], 0)
        return weights * (diagonal_coef * values + sign * swapped)

    def normal(values):
        first = brick_curl(values) + couple(values, 1.0, sigma)
        return (brick_curl(first) + couple(first, -1.0, sigma)) / norm_scale

    start = (brick_curl(spectrum) + couple(spectrum, -1.0, sigma)) / norm_scale
    carry_terms, push_terms, center = chebyshev_terms(SWEEPS - 1)

    def sweep(sweep_index, carry_state):
        current, residual, direction = carry_state
        current = current + direction
        residual = residual - normal(direction)
        direction = carry_terms[sweep_index] * direction + push_terms[sweep_index] * residual
        return (current, residual, direction)

    current, residual, direction = lax.fori_loop(
        0, SWEEPS - 1, sweep, (jnp.zeros_like(start), start, start / center)
    )
    solution = (current + direction).reshape(steps, groups, -1, depth_z)
    spread_back = jnp.einsum(
        "nk,kgrz->ngrz",
        inverse_table,
        lax.all_to_all(solution, "tm", split_axis=1, concat_axis=0, tiled=True),
        precision=lax.Precision.HIGHEST,
    )
    updated = lax.all_to_all(spread_back, "tm", split_axis=0, concat_axis=1, tiled=True)
    return updated.reshape(forcing.shape)


VMEM_BYTES = 63 * 1024 * 1024
AHEAD = 3
CHUNKS = 6


def pair_numbers(window, groups, spots):
    table = np.zeros((groups, spots), np.int64)
    for z in range(groups):
        for s in range(spots):
            table[z, s] = 2 * (spots * (z % 2) + s) + z // 2
    return table


def host_tables(window, groups, spots):
    steps = window // groups
    gamma = ALPHA ** (1.0 / window)
    pairs = pair_numbers(window, groups, spots)
    cas = lambda k, n: np.cos(2 * np.pi * ((k * n) % window) / window) + np.sin(
        2 * np.pi * ((k * n) % window) / window
    )
    rows = np.arange(steps)
    merge = np.zeros((groups, 2, steps))
    split = np.zeros((groups, 2, steps))
    ahead = np.zeros((groups, spots, 2, 2, steps))
    back = np.zeros((groups, 2, steps, spots, 2))
    for z in range(groups):
        mine, other = steps * z + rows, steps * ((z + 2) % 4) + rows
        upper = z // 2
        merge[z, 0] = (-1.0 if upper else 1.0) * gamma**mine
        merge[z, 1] = gamma**other
        split[z, 0] = (-1.0 if upper else 1.0) * gamma**-mine / window
        split[z, 1] = gamma**-mine / window
        for s in range(spots):
            j = pairs[z, s]
            for f, k in enumerate((j, window // 2 if j == 0 else window - j)):
                for side, low in enumerate((z % 2, 1 - z % 2)):
                    ahead[z, s, f, side] = cas(k, steps * low + rows)
                    back[z, side, :, s, f] = cas(k, steps * low + rows)
    theta = 2 * np.pi * pairs / window
    plain = 1 - gamma * np.cos(theta)
    p_plus = np.where(pairs == 0, 1 - gamma, plain)
    p_minus = np.where(pairs == 0, 1 + gamma, plain)
    cross = np.where(pairs == 0, 0.0, gamma * np.sin(theta))
    scale = (np.sqrt(np.maximum(p_plus, p_minus) ** 2 + cross**2) * SIGMA_TOP + CURL_TOP) ** 2
    coef = np.stack([p_plus, p_minus, cross, 1 / scale], -1)
    center, radius = (UPPER + LOWER) / 2, (UPPER - LOWER) / 2
    now, cheb = radius / center, []
    for _ in range(SWEEPS - 1):
        later = 1.0 / (2.0 * center / radius - now)
        cheb += [later * now, 2.0 * later / radius]
        now = later
    flat = [np.asarray(v, np.float32).reshape(-1) for v in (merge, ahead, coef, cheb, back, split)]
    offsets = np.cumsum([0] + [v.size for v in flat]).tolist()
    table = np.zeros(-(-offsets[-1] // 1024) * 1024, np.float32)
    table[: offsets[-1]] = np.concatenate(flat)
    return table, offsets, 1 / center


class Part:
    def __init__(self, ref, offset):
        self.ref, self.offset = ref, offset

    def __getitem__(self, index):
        return self.ref[index + self.offset]


def window_kernel(
    steps, spots, offsets, inverse_center,
    conductance_hbm, table_hbm, force_hbm, start_hbm, region_hbm, iterate_hbm, out_hbm,
    out, out_sem, conductance, table, force, start, region, latest, local_sem,
    got_last, got_far, mixed, got_near, extra, got_extra, mine_freq, spec, sigma,
    res, step, total, home, half, got_half, even, got_even,
    last_sem, far_sem, near_sem, extra_sem, sigma_sem, spec_sem, home_sem, half_sem, even_sem,
):
    z, s = lax.axis_index("tm"), lax.axis_index("space")
    far = ((z + 2) % 4, s)
    near = (z + 1 - 2 * (z % 2), s)
    peers = [(z, (s + hop) % spots) for hop in range(1, spots)]
    width = 6 // CHUNKS
    planes = 2 * spots
    parts = [pl.ds(c * width, width) for c in range(CHUNKS)]
    sent = []

    def send(source, target, sems, slot, device):
        copy = pltpu.make_async_remote_copy(
            src_ref=source, dst_ref=target,
            send_sem=sems.at[(0,) + slot], recv_sem=sems.at[(1,) + slot],
            device_id=device, device_id_type=pl.DeviceIdType.MESH,
        )
        copy.start()
        sent.append(copy)
        return copy

    barrier = pltpu.get_barrier_semaphore()
    for device in [far, near] + peers:
        pl.semaphore_signal(barrier, inc=1, device_id=device, device_id_type=pl.DeviceIdType.MESH)

    local = [
        pltpu.make_async_copy(source, target, local_sem.at[i])
        for i, (source, target) in enumerate([
            (region_hbm, region), (conductance_hbm, conductance), (table_hbm, table),
            (start_hbm, start), (iterate_hbm.at[steps - 1], latest),
            *[(force_hbm.at[:, i], force.at[i]) for i in range(6)],
        ])
    ]
    for copy in local:
        copy.start()
    merge, ahead, coef, cheb, back, split = [Part(table, offset) for offset in offsets[:-1]]
    local[0].wait()
    local[1].wait()
    material = region[...]
    brick_sigma = jnp.zeros(material.shape, jnp.float32)
    for index in range(3):
        brick_sigma = brick_sigma + jnp.where(material == index, conductance[index], 0.0)
    sigma[s] = brick_sigma
    pl.semaphore_wait(barrier, 2 + len(peers))

    last_copy = pltpu.make_async_remote_copy(
        src_ref=iterate_hbm.at[steps - 1], dst_ref=got_last,
        send_sem=last_sem.at[0], recv_sem=last_sem.at[1],
        device_id=far, device_id_type=pl.DeviceIdType.MESH,
    )

    @pl.when(z == 3)
    def _():
        last_copy.start()

    far_copies = []

    def send_far():
        c = len(far_copies)
        if c < CHUNKS:
            part = parts[c]
            for copy in local[5 + c * width : 5 + (c + 1) * width]:
                copy.wait()
            far_copies.append(send(force.at[part], got_far.at[part], far_sem, (c,), far))

    for _ in range(AHEAD):
        send_far()
    sigma_copies = [
        send(sigma.at[s], sigma.at[s], sigma_sem, (h,), peer) for h, peer in enumerate(peers)
    ]
    for copy in local[2:5]:
        copy.wait()
    extra[...] = jnp.zeros_like(extra)

    @pl.when(z == 1)
    def _():
        last_copy.wait_recv()
        extra[...] = got_last[...]

    @pl.when(z == 3)
    def _():
        last_copy.wait_send()
        extra[...] = latest[...]

    extra_copy = send(extra, got_extra, extra_sem, (0,), near)

    def mix(c):
        far_copies[c].wait_recv()
        send_far()

        def row(m, carry):
            w_mine, w_other = merge[z * 2 * steps + m], merge[(z * 2 + 1) * steps + m]
            for t in range(c * width, (c + 1) * width):
                mixed[t, m] = w_mine * force[t, m] + w_other * got_far[t, m]
            return carry

        lax.fori_loop(0, steps, row, 0, unroll=4)
        return send(mixed.at[parts[c]], got_near.at[parts[c]], near_sem, (c,), near)

    spec_copies = [None] * CHUNKS

    def transform(c, copy):
        copy.wait_recv()
        if c == 0:
            extra_copy.wait_recv()
            got_extra[...] = start[...] - ALPHA * (extra[...] + got_extra[...])
        jump = [brick_sigma[t % 2] * got_extra[t] for t in range(c * width, (c + 1) * width)]

        def slot(k, carry):
            base = (z * 2 * spots + k) * 2 * steps
            sums = [[j, None] for j in jump]
            for m in range(steps):
                w_mine, w_other = ahead[base + m], ahead[base + steps + m]
                for i in range(width):
                    t = c * width + i
                    term = w_other * got_near[t, m]
                    sums[i][0] = sums[i][0] + w_mine * mixed[t, m]
                    sums[i][1] = term if m == 0 else sums[i][1] + term
            for i in range(width):
                mine_freq[k // 2, c * width + i, k % 2] = sums[i][0] + sums[i][1]
            return carry

        lax.fori_loop(0, 2 * spots, slot, 0, unroll=4)
        spec[s, parts[c]] = mine_freq[s, parts[c]]
        spec_copies[c] = [
            send(mine_freq.at[peer[1], parts[c]], spec.at[s, parts[c]], spec_sem, (c, h), peer)
            for h, peer in enumerate(peers)
        ]

    pending = mix(0)
    for c in range(CHUNKS):
        later = mix(c + 1) if c + 1 < CHUNKS else None
        transform(c, pending)
        pending = later
    for copy in sigma_copies + [copy for group in spec_copies for copy in group]:
        copy.wait_recv()

    device = z * spots + s
    p_plus, p_minus = coef[device * 4], coef[device * 4 + 1]
    cross, inverse_scale = coef[device * 4 + 2], coef[device * 4 + 3]
    along_y = lax.broadcasted_iota(jnp.int32, (8, 128), 0)
    along_z = lax.broadcasted_iota(jnp.int32, (8, 128), 1)
    not_top_y, not_top_z = along_y < 7, along_z < 127
    not_low_y, not_low_z = along_y > 0, along_z > 0
    zero = jnp.zeros((8, 128), jnp.float32)

    def up_y(v):
        return jnp.where(not_top_y, pltpu.roll(v, 7, 0), 0.0)

    def up_z(v):
        return jnp.where(not_top_z, pltpu.roll(v, 127, 1), 0.0)

    def down_y(v):
        return jnp.where(not_low_y, pltpu.roll(v, 1, 0), 0.0)

    def down_z(v):
        return jnp.where(not_low_z, pltpu.roll(v, 1, 1), 0.0)

    def planes_of(buffer):
        return lambda i: [
            [buffer[i // 2, 2 * e + i % 2, f] for e in range(3)] for f in range(2)
        ]

    def operator(load, sign, finish):
        here = load(0)
        behind = [(zero, zero), (zero, zero)]
        for i in range(planes):
            ahead_field = load(i + 1) if i + 1 < planes else [[zero] * 3] * 2
            weight = sigma[i // 2, i % 2]
            weights = (weight * p_plus, weight * p_minus)
            weight_cross = weight * cross
            for f in range(2):
                ex, ey, ez = here[f]
                _, ey1, ez1 = ahead_field[f]
                bx = (up_y(ez) - ez) - (up_z(ey) - ey)
                by = (up_z(ex) - ex) - (ez1 - ez)
                bz = (ey1 - ey) - (up_y(ex) - ex)
                by0, bz0 = behind[f]
                curls = (
                    (down_z(by) - by) - (down_y(bz) - bz),
                    (bz0 - bz) - (down_z(bx) - bx),
                    (down_y(bx) - bx) - (by0 - by),
                )
                behind[f] = (by, bz)
                for e in range(3):
                    own = weights[f] * here[f][e]
                    swapped = weight_cross * here[1 - f][e]
                    value = curls[e] + own
                    value = value + swapped if (f == 1) == (sign > 0) else value - swapped
                    finish(i, e, f, value)
            here = ahead_field
            yield

    def begin(i, e, f, value):
        at = (i // 2, 2 * e + i % 2, f)
        res[at] = value
        moved = value * (inverse_scale * inverse_center)
        step[at] = moved
        total[at] = moved

    for _ in operator(planes_of(spec), -1.0, begin):
        pass

    def sweep_passes(index):
        w_step, w_res = cheb[index * 2], cheb[index * 2 + 1] * inverse_scale
        first = [[[None] * 3 for _ in range(2)] for _ in range(planes)]

        def keep(i, e, f, value):
            first[i][f][e] = value

        def advance(i, e, f, value):
            at = (i // 2, 2 * e + i % 2, f)
            new = res[at] - value
            res[at] = new
            moved = w_step * step[at] + w_res * new
            step[at] = moved
            total[at] = total[at] + moved

        return [
            operator(planes_of(step), 1.0, keep),
            operator(lambda i: first[i], -1.0, advance),
        ]

    def sweeps(indices):
        passes = [one for index in indices for one in sweep_passes(index)]
        for tick in range(planes + len(passes) - 1):
            for lag, one in enumerate(passes):
                if 0 <= tick - lag < planes:
                    next(one)

    def two_sweeps(index, carry):
        sweeps([2 * index, 2 * index + 1])
        return carry

    lax.fori_loop(0, (SWEEPS - 1) // 2, two_sweeps, 0)
    if (SWEEPS - 1) % 2:
        sweeps([SWEEPS - 2])

    home_copies = []

    def send_home():
        c = len(home_copies)
        if c == CHUNKS:
            return
        part = parts[c]
        home[s, part] = total[s, part]
        home_copies.append([
            send(total.at[peer[1], part], home.at[s, part], home_sem, (c, h), peer)
            for h, peer in enumerate(peers)
        ])

    def gather(c):
        for copy in home_copies[c]:
            copy.wait_recv()

        def row(m, carry):
            base_mine = (z * 2 * steps + m) * 2 * spots
            base_other = ((z * 2 + 1) * steps + m) * 2 * spots
            for t in range(c * width, (c + 1) * width):
                mine, other = [None, None], [None, None]
                for b in range(spots):
                    for f in range(2):
                        value = home[b, t, f]
                        term = back[base_mine + 2 * b + f] * value
                        mine[f] = term if b == 0 else mine[f] + term
                        term = back[base_other + 2 * b + f] * value
                        other[f] = term if b == 0 else other[f] + term
                even[t, m] = mine[0] + mine[1]
                half[t, m] = other[0] + other[1]
            return carry

        lax.fori_loop(0, steps, row, 0, unroll=4)
        return send(half.at[parts[c]], got_half.at[parts[c]], half_sem, (c,), near)

    def add(c, copy):
        copy.wait_recv()
        even[parts[c]] = even[parts[c]] + got_half[parts[c]]
        return send(even.at[parts[c]], got_even.at[parts[c]], even_sem, (c,), far)

    send_home()
    send_home()
    half_copies = [gather(0)]
    send_home()
    even_copies, out_copies = [], []
    for c in range(CHUNKS):
        if c + 1 < CHUNKS:
            half_copies.append(gather(c + 1))
            send_home()
        even_copies.append(add(c, half_copies[c]))
    for c in range(CHUNKS):
        even_copies[c].wait_recv()

        def row(m, carry):
            w_mine, w_other = split[z * 2 * steps + m], split[(z * 2 + 1) * steps + m]
            for t in range(c * width, (c + 1) * width):
                out[t, m] = w_mine * even[t, m] + w_other * got_even[t, m]
            return carry

        lax.fori_loop(0, steps, row, 0, unroll=4)
        for t in range(c * width, (c + 1) * width):
            out_copies.append(pltpu.make_async_copy(out.at[t], out_hbm.at[:, t], out_sem.at[t]))
            out_copies[t].start()
    for copy in sent:
        copy.wait_send()
    for copy in out_copies:
        copy.wait()


def pair_per_device(groups, spots, forcing, start_field, iterate, region, conductance):
    steps = forcing.shape[0]
    table, offsets, inverse_center = host_tables(steps * groups, groups, spots)
    tile = forcing.shape[3:]
    f32 = jnp.float32
    brick = lambda *lead: pltpu.VMEM(lead + tile, f32)
    rows = brick(6, steps)
    grid = brick(spots, 6, 2)
    dma = pltpu.SemaphoreType.DMA
    hbm = pl.BlockSpec(memory_space=pl.ANY)
    result = pl.pallas_call(
        functools.partial(window_kernel, steps, spots, offsets, inverse_center),
        out_shape=jax.ShapeDtypeStruct((steps, 6) + tile, f32),
        in_specs=[hbm] * 6,
        out_specs=hbm,
        scratch_shapes=[
            rows, dma((6,)), pltpu.SMEM(conductance.shape, f32), pltpu.SMEM(table.shape, f32), rows, brick(6), pltpu.VMEM(region.shape, region.dtype),
            brick(6), dma((11,)),
            brick(6), rows, rows, rows, brick(6), brick(6), grid, grid, brick(spots, 2),
            grid, grid, grid, grid, rows, rows, rows, rows,
            dma((2,)), dma((2, CHUNKS)), dma((2, CHUNKS)), dma((2, 1)), dma((2, spots - 1)),
            dma((2, CHUNKS, spots - 1)), dma((2, CHUNKS, spots - 1)),
            dma((2, CHUNKS)), dma((2, CHUNKS)),
        ],
        compiler_params=pltpu.CompilerParams(
            collective_id=0, has_side_effects=True, vmem_limit_bytes=VMEM_BYTES
        ),
    )(
        conductance, jnp.asarray(table),
        forcing.reshape((steps, 6) + tile), start_field.reshape((6,) + tile), region,
        iterate.reshape((steps, 6) + tile),
    )
    return result.reshape(forcing.shape)


def solution(mesh):
    placed = (
        P("tm", None, "space", None, None),
        P(None, "space", None, None),
        P("tm", None, "space", None, None),
        P("space", None, None),
        P(),
    )
    groups, spots = mesh.shape["tm"], mesh.shape["space"]

    def per_block(*arrays):
        steps, planes = arrays[0].shape[0], arrays[0].shape[2]
        one_each = steps * groups == 2 * groups * spots
        if groups == 4 and one_each and planes == 2 and arrays[0].shape[3:] == (8, 128):
            return pair_per_device(groups, spots, *arrays)
        return per_device(*arrays)

    return jax.shard_map(
        per_block,
        mesh=mesh,
        in_specs=placed,
        out_specs=P("tm", None, "space", None, None),
        check_vma=False,
    )
```
